512 devices in a mesh: dp: 16 (over z), label: 32 (over y, x, core).
Axes of the slice: x: 4, y: 4, z: 16, core: 2. Of those that a mesh axis runs over, the one named last changes fastest.
Arguments:
- queries: bfloat16 [8192, 768], P('dp')
- embeddings: bfloat16 [16384, 768], P('label')
- shortlist: int32 [64, 48], P('dp'), may hold values from 0 to 127, as said below
- positive: int32 [8192], P('dp'), may hold values from 0 to 16383, as said below
Outputs:
- losses: float32 [8192], P('dp')
- query_grad: bfloat16 [8192, 768], P('dp')
- label_grad: float32 [128, 128, 768], P('dp', 'label')
The draws below stay inside these ranges and needn't reach their ends.
Inputs may be any that keep to these rules, and one draw needn't show every extreme that they name: `shortlist`: each row lists 48 different label blocks. `shortlist`: of the blocks listed for one query block, at most 3 lie among the 4 blocks b with the same b // 4, and every row reaches 3 for some such group; for every even query block that group is b // 4 == 16. Each query's positive label lies in one of the blocks listed for its query block.
All inputs are finite; a program needn't handle non-finite values.
Results may differ from the reference program's by a relative error of at most 0.0037.
Values may be sent and summed in bfloat16 or wider, within the bound.
No kernel may reach another device: no remote copies, remote signals or barrier semaphores. Data moves between devices by JAX's collectives and lax.ppermute only.
A program may use at most 64 MiB of HBM per device.

```python
import jax
import jax.numpy as jnp
from jax import lax

D = 768
BLOCK = 128
LB_DEV = 4
SHORT = 48
HITS = 3
QUERIES = 8192
LABELS = 16384
QBLOCKS = 64
LBLOCKS = 128


def shortlist_ids(key):
    owners = LBLOCKS // LB_DEV
    slots = owners * HITS
    popular = jax.random.randint(jax.random.fold_in(key, 101), (owners,), 0, 4 * slots)
    jitter = jax.random.randint(jax.random.fold_in(key, 102), (QBLOCKS, owners, HITS), 0, 8 * slots)
    drawn_owner = jax.random.randint(jax.random.fold_in(key, 104), (QBLOCKS,), 0, owners)
    even_rows = jnp.arange(QBLOCKS, dtype=jnp.int32) % 2 == 0
    forced = jnp.where(even_rows, owners // 2, drawn_owner).astype(jnp.int32)
    boost = jnp.where(jnp.arange(owners, dtype=jnp.int32)[None, :] == forced[:, None], 16 * slots, 0)
    score = popular[None, :, None] + jitter + boost[:, :, None]
    ranking = score.reshape(QBLOCKS, slots) * slots + jnp.arange(slots, dtype=jnp.int32)[None, :]
    chosen = lax.top_k(ranking, SHORT)[1].astype(jnp.int32)
    owner = chosen // HITS
    within = chosen % HITS
    base = jax.random.randint(jax.random.fold_in(key, 105), (QBLOCKS, owners), 0, LB_DEV)
    offset = (jnp.take_along_axis(base, owner, axis=1) + within) % LB_DEV
    return (owner * LB_DEV + offset).astype(jnp.int32)


def draw_shortlist(key, part):
    return shortlist_ids(key)


def draw_positive(key, part):
    listed = shortlist_ids(key)
    key = jax.random.fold_in(key, 7)
    picked = jax.random.randint(jax.random.fold_in(key, 1), (QUERIES,), 0, SHORT)
    inside = jax.random.randint(jax.random.fold_in(key, 2), (QUERIES,), 0, BLOCK)
    owners = jnp.arange(QUERIES, dtype=jnp.int32) // BLOCK
    return (listed[owners, picked] * BLOCK + inside).astype(jnp.int32)


def draw_queries(key, part):
    key = jax.random.fold_in(key, 11)
    values = jnp.clip(jax.random.normal(jax.random.fold_in(key, 1), (QUERIES, D), jnp.float32), -6.0, 6.0)
    return values.astype(jnp.bfloat16)


def draw_embeddings(key, part):
    key = jax.random.fold_in(key, 13)
    spread = 3.0 / D ** 0.5
    values = jnp.clip(jax.random.normal(jax.random.fold_in(key, 1), (LABELS, D), jnp.float32), -6.0, 6.0) * spread
    return values.astype(jnp.bfloat16)


def setup_inputs(seed: int = 0) -> dict:
    key_of = jax.random.split(jax.random.key(seed), 5)
    queries = draw_queries(jax.random.fold_in(key_of[4], 71), 0)
    embeddings = draw_embeddings(jax.random.fold_in(key_of[4], 71), 0)
    shortlist = draw_shortlist(jax.random.fold_in(key_of[4], 71), 0)
    positive = draw_positive(jax.random.fold_in(key_of[4], 71), 0)
    return {"queries": queries, "embeddings": embeddings, "shortlist": shortlist, "positive": positive}


def reference(queries, embeddings, shortlist, positive):
    label_count = embeddings.shape[0]
    block_of = jnp.arange(label_count, dtype=jnp.int32) // BLOCK
    columns = jnp.arange(label_count, dtype=jnp.int32)
    all_blocks = jnp.arange(LBLOCKS, dtype=jnp.int32)

    def step(accumulated, block_index):
        begin_row = (block_index * BLOCK).astype(jnp.int32)
        block_rows = lax.dynamic_slice_in_dim(queries, begin_row, BLOCK, 0)
        block_positive = lax.dynamic_slice_in_dim(positive, begin_row, BLOCK, 0)
        listed = lax.dynamic_index_in_dim(shortlist, block_index, 0, keepdims=False)
        chosen = jnp.any(listed[:, None] == all_blocks[None, :], axis=0)
        selected = chosen[block_of]
        scores = jnp.dot(block_rows, embeddings.T, preferred_element_type=jnp.float32)
        masked = jnp.where(selected[None, :], scores, -jnp.inf)
        row_top = jnp.max(masked, axis=1, keepdims=True)
        weights = jnp.exp(masked - row_top)
        row_total = jnp.sum(weights, axis=1, keepdims=True)
        is_positive = columns[None, :] == block_positive[:, None]
        positive_score = jnp.sum(jnp.where(is_positive, scores, 0.0), axis=1)
        losses = row_top[:, 0] + jnp.log(row_total[:, 0]) - positive_score
        gradient = (weights / row_total - is_positive.astype(jnp.float32)).astype(jnp.bfloat16)
        query_part = jnp.dot(gradient, embeddings, preferred_element_type=jnp.float32).astype(jnp.bfloat16)
        accumulated = accumulated + jnp.dot(gradient.T, block_rows, preferred_element_type=jnp.float32)
        return accumulated, (losses, query_part)

    start_sum = jnp.zeros((label_count, D), jnp.float32)
    accumulated, (losses, query_parts) = lax.scan(step, start_sum, jnp.arange(QBLOCKS, dtype=jnp.int32))
    label_grad = accumulated.reshape(LBLOCKS, BLOCK, D).transpose(1, 0, 2)
    return losses.reshape(-1), query_parts.reshape(-1, D), label_grad
```

```python
import functools

import jax
import jax.numpy as jnp
from jax import lax
from jax.experimental import pallas as pl
from jax.experimental.pallas import tpu as pltpu
from jax.sharding import PartitionSpec as P

BLOCK = 128
LOWEST = -3.4028234e38
VMEM_LIMIT = 32 * 1024 * 1024
F32 = jnp.float32
BF16 = jnp.bfloat16


def call(kernel, out_shape, args, flops=0, smem=0, scratch=(), moved=2_000_000):
    specs = [pl.BlockSpec(memory_space=pltpu.SMEM)] * smem
    specs += [pl.BlockSpec(memory_space=pltpu.VMEM)] * (len(args) - smem)
    return pl.pallas_call(
        kernel,
        out_shape=out_shape,
        in_specs=specs,
        out_specs=jax.tree.map(lambda _: pl.BlockSpec(memory_space=pltpu.VMEM), out_shape),
        scratch_shapes=list(scratch),
        compiler_params=pltpu.CompilerParams(vmem_limit_bytes=VMEM_LIMIT),
        cost_estimate=pl.CostEstimate(flops=flops, bytes_accessed=moved, transcendentals=0),
    )(*args)


def local_scores(me, short_ref, positive_ref, queries_ref, embeddings_ref):
    labels, rows = embeddings_ref.shape[0], queries_ref.shape[0]
    label_blocks, query_blocks = labels // BLOCK, rows // BLOCK
    scores = lax.dot_general(
        embeddings_ref[...], queries_ref[...], (((1,), (1,)), ((), ())), preferred_element_type=F32
    )
    listed = short_ref[...]
    masked = []
    for b in range(label_blocks):
        hit = jnp.max(
            jnp.where(listed == me * label_blocks + b, 1.0, 0.0).astype(F32), axis=1, keepdims=True
        )
        row = jnp.concatenate(
            [jnp.broadcast_to(hit[q : q + 1], (1, BLOCK)) for q in range(query_blocks)], axis=1
        )
        masked.append(jnp.where(row > 0.5, scores[b * BLOCK : (b + 1) * BLOCK], -jnp.inf))
    masked = jnp.concatenate(masked, axis=0)
    place = positive_ref[...] - me * labels
    is_positive = lax.broadcasted_iota(jnp.int32, (labels, rows), 0) == place
    return scores, masked, is_positive


def stats_kernel(short_ref, positive_ref, queries_ref, embeddings_ref, out_ref):
    me = lax.axis_index("label")
    scores, masked, is_positive = local_scores(
        me, short_ref, positive_ref, queries_ref, embeddings_ref
    )
    top = jnp.maximum(jnp.max(masked, axis=0, keepdims=True), LOWEST)
    total = jnp.sum(jnp.exp(masked - top), axis=0, keepdims=True)
    positive = jnp.sum(jnp.where(is_positive, scores, 0.0), axis=0, keepdims=True)
    rows = jnp.concatenate([top, total, positive, jnp.zeros_like(top)], axis=0)
    out_ref[...] = jnp.broadcast_to(rows[None], out_ref.shape)


def gradient_kernel(
    short_ref, positive_ref, stats_ref, queries_ref, embeddings_ref, loss_ref, grad_ref, label_ref
):
    me = lax.axis_index("label")
    tops, totals = stats_ref[:, 0, :], stats_ref[:, 1, :]
    top = jnp.max(tops, axis=0, keepdims=True)
    total = jnp.sum(totals * jnp.exp(tops - top), axis=0, keepdims=True)
    positive = jnp.sum(stats_ref[:, 2, :], axis=0, keepdims=True)
    loss_ref[...] = top + jnp.log(total) - positive
    _, masked, is_positive = local_scores(me, short_ref, positive_ref, queries_ref, embeddings_ref)
    weights = jnp.exp(masked - top) * (1.0 / total)
    gradient = jnp.where(is_positive, weights - 1.0, weights).astype(BF16)
    grad_ref[...] = gradient
    part = jnp.dot(gradient, queries_ref[...], preferred_element_type=F32)
    parts = label_ref.shape[0]
    blocks = part.shape[0] // BLOCK
    deep = BLOCK // parts
    width = part.shape[1]
    part = part.reshape(blocks, parts, deep, width)
    for p in range(parts):
        label_ref[p] = part[:, p].reshape(blocks * deep, width).astype(BF16)


def query_kernel(grad_ref, embeddings_ref, out_ref):
    out_ref[...] = lax.dot_general(
        grad_ref[...], embeddings_ref[...], (((0,), (0,)), ((), ())), preferred_element_type=F32
    ).astype(BF16)


def spread_kernel(parts_ref, out_ref):
    total = parts_ref[0].astype(F32)
    for i in range(1, parts_ref.shape[0]):
        total = total + parts_ref[i].astype(F32)
    out_ref[...] = jnp.broadcast_to(total.astype(BF16)[None], out_ref.shape)


def body(queries, embeddings, shortlist, positive):
    rows, width = queries.shape
    labels = embeddings.shape[0]
    groups, planes = lax.axis_size("label"), lax.axis_size("dp")
    shape = jax.ShapeDtypeStruct
    positive = positive.reshape(1, rows)
    madds = rows * labels * width

    stats = call(
        stats_kernel,
        shape((groups, 4, rows), F32),
        (shortlist, positive, queries, embeddings),
        flops=2 * madds,
    )
    stats = lax.all_to_all(stats, "label", 0, 0)
    losses, gradient, label_part = call(
        gradient_kernel,
        (
            shape((1, rows), F32),
            shape((labels, rows), BF16),
            shape((planes, labels // planes, width), BF16),
        ),
        (shortlist, positive, stats, queries, embeddings),
        flops=4 * madds,
    )
    label_parts = lax.all_to_all(label_part, "dp", 0, 0)
    query_part = call(query_kernel, shape((rows, width), BF16), (gradient, embeddings), flops=2 * madds)
    query_parts = lax.all_to_all(
        query_part.reshape(groups, rows // groups, width), "label", 0, 0
    )
    chunk = call(spread_kernel, shape(query_parts.shape, BF16), (query_parts,))
    query_grad = lax.all_to_all(chunk, "label", 0, 0).reshape(rows, width)
    label_grad = jnp.sum(label_parts.astype(F32), axis=0)
    label_grad = label_grad.reshape(labels // BLOCK, BLOCK // planes, width).swapaxes(0, 1)
    return losses.reshape(rows), query_grad, label_grad


def solution(mesh):
    in_specs = (P("dp", None), P("label", None), P("dp", None), P("dp"))
    out_specs = (P("dp"), P("dp", None), P("dp", "label", None))
    return jax.shard_map(body, mesh=mesh, in_specs=in_specs, out_specs=out_specs, check_vma=False)
```

```python
import jax
import jax.numpy as jnp
from jax import lax
from jax.experimental import pallas as pl
from jax.experimental.pallas import tpu as pltpu
from jax.sharding import PartitionSpec as P

BLOCK = 128
LOWEST = -3.4028234e38
VMEM_LIMIT = 24 * 1024 * 1024
VMEM_MOST = 62_000_000
F32 = jnp.float32
BF16 = jnp.bfloat16


def call(kernel, out_shape, args, flops=0, scratch=(), any_inputs=0, vmem=VMEM_LIMIT):
    specs = [pl.BlockSpec(memory_space=pltpu.HBM)] * any_inputs
    specs += [pl.BlockSpec(memory_space=pltpu.VMEM)] * (len(args) - any_inputs)
    return pl.pallas_call(
        kernel,
        out_shape=out_shape,
        in_specs=specs,
        out_specs=jax.tree.map(lambda _: pl.BlockSpec(memory_space=pltpu.VMEM), out_shape),
        scratch_shapes=list(scratch),
        compiler_params=pltpu.CompilerParams(vmem_limit_bytes=vmem),
        cost_estimate=pl.CostEstimate(flops=flops, bytes_accessed=2_000_000, transcendentals=0),
    )(*args)


def local_scores(me, short_ref, positive_ref, queries_ref, embeddings_ref):
    labels, rows = embeddings_ref.shape[0], queries_ref.shape[0]
    label_blocks, query_blocks = labels // BLOCK, rows // BLOCK
    scores = lax.dot_general(
        embeddings_ref[...], queries_ref[...], (((1,), (1,)), ((), ())), preferred_element_type=F32
    )
    listed = short_ref[...]
    masked = []
    for b in range(label_blocks):
        hit = jnp.max(
            jnp.where(listed == me * label_blocks + b, 1.0, 0.0).astype(F32), axis=1, keepdims=True
        )
        row = jnp.concatenate(
            [jnp.broadcast_to(hit[q : q + 1], (1, BLOCK)) for q in range(query_blocks)], axis=1
        )
        masked.append(jnp.where(row > 0.5, scores[b * BLOCK : (b + 1) * BLOCK], -jnp.inf))
    masked = jnp.concatenate(masked, axis=0)
    place = positive_ref[...] - me * labels
    is_positive = lax.broadcasted_iota(jnp.int32, (labels, rows), 0) == place
    return scores, masked, is_positive


def stats_kernel(
    short_hbm, positive_hbm, queries_hbm, embeddings_hbm, out_ref,
    short_ref, positive_ref, queries_ref, embeddings_ref, sems,
):
    copies = [
        pltpu.make_async_copy(source, target, sems.at[i])
        for i, (source, target) in enumerate(
            [
                (queries_hbm, queries_ref),
                (embeddings_hbm, embeddings_ref),
                (short_hbm, short_ref),
                (positive_hbm, positive_ref),
            ]
        )
    ]
    for copy in copies:
        copy.start()
    for copy in copies:
        copy.wait()
    me = lax.axis_index("label")
    scores, masked, is_positive = local_scores(
        me, short_ref, positive_ref, queries_ref, embeddings_ref
    )
    top = jnp.maximum(jnp.max(masked, axis=0, keepdims=True), LOWEST)
    total = jnp.sum(jnp.exp(masked - top), axis=0, keepdims=True)
    positive = jnp.sum(jnp.where(is_positive, scores, 0.0), axis=0, keepdims=True)
    rows = jnp.concatenate([top + jnp.log(total), positive], axis=0)
    out_ref[...] = jnp.broadcast_to(rows[None], out_ref.shape)


def gradient_kernel(
    short_ref, positive_ref, stats_ref, queries_ref, embeddings_ref,
    loss_ref, grad_ref, keep_ref, right_ref, left_ref, far_ref, part_ref,
):
    me = lax.axis_index("label")
    logs = stats_ref[:, 0, :]
    top = jnp.max(logs, axis=0, keepdims=True)
    log_total = top + jnp.log(jnp.sum(jnp.exp(logs - top), axis=0, keepdims=True))
    positive = jnp.sum(stats_ref[:, 1, :], axis=0, keepdims=True)
    loss_ref[...] = log_total - positive
    _, masked, is_positive = local_scores(me, short_ref, positive_ref, queries_ref, embeddings_ref)
    weights = jnp.exp(masked - log_total)
    gradient = jnp.where(is_positive, weights - 1.0, weights).astype(BF16)
    grad_ref[...] = gradient
    part_ref[...] = jnp.dot(gradient, queries_ref[...], preferred_element_type=F32)
    plane = lax.axis_index("dp")
    labels = part_ref.shape[0]
    deep = BLOCK // lax.axis_size("dp")
    blocks = labels // BLOCK
    for ref, shift in ((keep_ref, 0), (right_ref, 1), (left_ref, 3), (far_ref, 2)):
        kind = lax.rem(plane + shift, 4)
        for m in range(ref.shape[0]):
            start = pl.multiple_of((4 * m + kind) * deep, deep)
            rows = [part_ref[pl.ds(b * BLOCK + start, deep), :] for b in range(blocks)]
            ref[m] = jnp.concatenate(rows, axis=0).astype(ref.dtype)


def query_kernel(grad_ref, embeddings_ref, out_ref):
    out_ref[...] = lax.dot_general(
        grad_ref[...], embeddings_ref[...], (((0,), (0,)), ((), ())), preferred_element_type=F32
    ).astype(BF16)


def middle_kernel(
    parts_ref, a_ref, b_ref, c_ref, d_ref, spread_ref, keep_ref, right_ref, left_ref, far_ref
):
    total = parts_ref[0].astype(F32)
    for i in range(1, parts_ref.shape[0]):
        total = total + parts_ref[i].astype(F32)
    spread_ref[...] = jnp.broadcast_to(total.astype(BF16)[None], spread_ref.shape)
    mine = lax.axis_index("dp") // 4
    for ref, shift in ((keep_ref, 0), (right_ref, 1), (left_ref, 3), (far_ref, 2)):
        m = lax.rem(mine + shift, 4)
        total = a_ref[m] + b_ref[m].astype(F32) + c_ref[m].astype(F32) + d_ref[m].astype(F32)
        ref[...] = total.astype(ref.dtype)


def last_kernel(a_ref, b_ref, c_ref, d_ref, out_ref):
    total = a_ref[...] + b_ref[...].astype(F32) + c_ref[...].astype(F32) + d_ref[...].astype(F32)
    deep, blocks = out_ref.shape[:2]
    for b in range(blocks):
        out_ref[:, b, :] = total[b * deep : (b + 1) * deep]


def moved_by(x, shift):
    planes = lax.axis_size("dp")
    return lax.ppermute(x, "dp", [(i, (i + shift) % planes) for i in range(planes)])


def body(queries, embeddings, shortlist, positive):
    rows, width = queries.shape
    labels = embeddings.shape[0]
    groups, planes = lax.axis_size("label"), lax.axis_size("dp")
    shape = jax.ShapeDtypeStruct
    positive = positive.reshape(1, rows)
    madds = rows * labels * width
    chunk = labels // planes

    given = (shortlist, positive, queries, embeddings)
    stats = call(
        stats_kernel,
        shape((groups, 2, rows), F32),
        given,
        flops=2 * madds,
        scratch=[pltpu.VMEM(x.shape, x.dtype) for x in given] + [pltpu.SemaphoreType.DMA((4,))],
        any_inputs=4,
        vmem=VMEM_MOST,
    )
    stats = lax.all_to_all(stats, "label", 0, 0)
    losses, gradient, keep, right, left, far = call(
        gradient_kernel,
        (
            shape((1, rows), F32),
            shape((labels, rows), BF16),
            shape((planes // 4, chunk, width), F32),
        )
        + (shape((planes // 4, chunk, width), BF16),) * 3,
        (shortlist, positive, stats, queries, embeddings),
        flops=4 * madds,
        scratch=(pltpu.VMEM((labels, width), F32),),
    )
    right, left, far = moved_by(right, 1), moved_by(left, -1), moved_by(far, 2)
    query_part = call(query_kernel, shape((rows, width), BF16), (gradient, embeddings), flops=2 * madds)
    query_parts = lax.all_to_all(
        query_part.reshape(groups, rows // groups, width), "label", 0, 0
    )
    spread, keep, right, left, far = call(
        middle_kernel,
        (shape(query_parts.shape, BF16), shape((chunk, width), F32))
        + (shape((chunk, width), BF16),) * 3,
        (query_parts, keep, right, left, far),
    )
    query_grad = lax.all_to_all(spread, "label", 0, 0).reshape(rows, width)
    right, left, far = moved_by(right, 4), moved_by(left, -4), moved_by(far, 8)
    label_grad = call(
        last_kernel,
        shape((BLOCK // planes, labels // BLOCK, width), F32),
        (keep, right, left, far),
    )
    return losses.reshape(rows), query_grad, label_grad


def solution(mesh):
    in_specs = (P("dp", None), P("label", None), P("dp", None), P("dp"))
    out_specs = (P("dp"), P("dp", None), P("dp", "label", None))
    return jax.shard_map(body, mesh=mesh, in_specs=in_specs, out_specs=out_specs, check_vma=False)
```

```python
import jax
import jax.numpy as jnp
from jax import lax
from jax.experimental import pallas as pl
from jax.experimental.pallas import tpu as pltpu
from jax.sharding import PartitionSpec as P

BLOCK = 128
LOWEST = -3.4028234e38
VMEM_LIMIT = 24 * 1024 * 1024
VMEM_MOST = 62_000_000
F32 = jnp.float32
BF16 = jnp.bfloat16


def call(kernel, out_shape, args, flops=0, scratch=(), any_inputs=0, any_outputs=0, vmem=VMEM_LIMIT):
    specs = [pl.BlockSpec(memory_space=pltpu.HBM)] * any_inputs
    specs += [pl.BlockSpec(memory_space=pltpu.VMEM)] * (len(args) - any_inputs)
    results = [pl.BlockSpec(memory_space=pltpu.VMEM)] * (len(out_shape) - any_outputs)
    results += [pl.BlockSpec(memory_space=pltpu.HBM)] * any_outputs
    return pl.pallas_call(
        kernel,
        out_shape=out_shape,
        in_specs=specs,
        out_specs=tuple(results),
        scratch_shapes=list(scratch),
        compiler_params=pltpu.CompilerParams(vmem_limit_bytes=vmem),
        cost_estimate=pl.CostEstimate(flops=flops, bytes_accessed=2_000_000, transcendentals=0),
    )(*args)


def local_scores(me, short_ref, positive_ref, queries_ref, embeddings_ref):
    labels, rows = embeddings_ref.shape[0], queries_ref.shape[0]
    label_blocks, query_blocks = labels // BLOCK, rows // BLOCK
    scores = lax.dot_general(
        embeddings_ref[...], queries_ref[...], (((1,), (1,)), ((), ())), preferred_element_type=F32
    )
    listed = short_ref[...]
    masked = []
    for b in range(label_blocks):
        hit = jnp.max(
            jnp.where(listed == me * label_blocks + b, 1.0, 0.0).astype(F32), axis=1, keepdims=True
        )
        row = jnp.concatenate(
            [jnp.broadcast_to(hit[q : q + 1], (1, BLOCK)) for q in range(query_blocks)], axis=1
        )
        masked.append(jnp.where(row > 0.5, scores[b * BLOCK : (b + 1) * BLOCK], -jnp.inf))
    masked = jnp.concatenate(masked, axis=0)
    place = positive_ref[...] - me * labels
    is_positive = lax.broadcasted_iota(jnp.int32, (labels, rows), 0) == place
    return scores, masked, is_positive


def stats_kernel(
    short_hbm, positive_hbm, queries_hbm, embeddings_hbm, out_ref,
    short_ref, positive_ref, queries_ref, embeddings_ref, sems,
):
    copies = [
        pltpu.make_async_copy(source, target, sems.at[i])
        for i, (source, target) in enumerate(
            [
                (queries_hbm, queries_ref),
                (embeddings_hbm, embeddings_ref),
                (short_hbm, short_ref),
                (positive_hbm, positive_ref),
            ]
        )
    ]
    for copy in copies:
        copy.start()
    for copy in copies:
        copy.wait()
    me = lax.axis_index("label")
    scores, masked, is_positive = local_scores(
        me, short_ref, positive_ref, queries_ref, embeddings_ref
    )
    top = jnp.maximum(jnp.max(masked, axis=0, keepdims=True), LOWEST)
    total = jnp.sum(jnp.exp(masked - top), axis=0, keepdims=True)
    positive = jnp.sum(jnp.where(is_positive, scores, 0.0), axis=0, keepdims=True)
    rows = jnp.concatenate([top + jnp.log(total), positive], axis=0)
    out_ref[...] = jnp.broadcast_to(rows[None], out_ref.shape)


def gradient_kernel(
    short_ref, positive_ref, stats_ref, queries_ref, embeddings_ref,
    loss_ref, query_ref, keep_ref, right_ref, left_ref, far_ref, part_ref,
):
    me = lax.axis_index("label")
    logs = stats_ref[:, 0, :]
    top = jnp.max(logs, axis=0, keepdims=True)
    log_total = top + jnp.log(jnp.sum(jnp.exp(logs - top), axis=0, keepdims=True))
    positive = jnp.sum(stats_ref[:, 1, :], axis=0, keepdims=True)
    loss_ref[...] = log_total - positive
    _, masked, is_positive = local_scores(me, short_ref, positive_ref, queries_ref, embeddings_ref)
    weights = jnp.exp(masked - log_total)
    gradient = jnp.where(is_positive, weights - 1.0, weights).astype(BF16)
    part_ref[...] = jnp.dot(gradient, queries_ref[...], preferred_element_type=F32)
    plane = lax.axis_index("dp")
    labels = part_ref.shape[0]
    deep = BLOCK // lax.axis_size("dp")
    blocks = labels // BLOCK
    for ref, shift in ((keep_ref, 0), (right_ref, 1), (left_ref, 3), (far_ref, 2)):
        kind = lax.rem(plane + shift, 4)
        for m in range(ref.shape[0]):
            start = pl.multiple_of((4 * m + kind) * deep, deep)
            rows = [part_ref[pl.ds(b * BLOCK + start, deep), :] for b in range(blocks)]
            ref[m] = jnp.concatenate(rows, axis=0).astype(ref.dtype)
    query_ref[...] = lax.dot_general(
        gradient, embeddings_ref[...], (((0,), (0,)), ((), ())), preferred_element_type=F32
    ).astype(BF16)


def middle_kernel(
    parts_ref, a_ref, b_ref, c_ref, d_ref, spread_ref, keep_ref, right_ref, left_ref, far_ref
):
    total = parts_ref[0].astype(F32)
    for i in range(1, parts_ref.shape[0]):
        total = total + parts_ref[i].astype(F32)
    spread_ref[...] = jnp.broadcast_to(total.astype(BF16)[None], spread_ref.shape)
    mine = lax.axis_index("dp") // 4
    for ref, shift in ((keep_ref, 0), (right_ref, 1), (left_ref, 3), (far_ref, 2)):
        m = lax.rem(mine + shift, 4)
        total = a_ref[m] + b_ref[m].astype(F32) + c_ref[m].astype(F32) + d_ref[m].astype(F32)
        ref[...] = total.astype(ref.dtype)


def last_kernel(a_ref, b_ref, c_ref, d_ref, query_ref, label_ref, query_hbm, sem):
    copy = pltpu.make_async_copy(query_ref, query_hbm, sem)
    copy.start()
    total = a_ref[...] + b_ref[...].astype(F32) + c_ref[...].astype(F32) + d_ref[...].astype(F32)
    deep, blocks = label_ref.shape[:2]
    for b in range(blocks):
        label_ref[:, b, :] = total[b * deep : (b + 1) * deep]
    copy.wait()


def moved_by(x, shift):
    planes = lax.axis_size("dp")
    return lax.ppermute(x, "dp", [(i, (i + shift) % planes) for i in range(planes)])


def moved_by_two(x):
    planes = lax.axis_size("dp")
    return lax.ppermute(x, "dp", [(i, (i + 2 - i % 2 * 4) % planes) for i in range(planes)])


def body(queries, embeddings, shortlist, positive):
    rows, width = queries.shape
    labels = embeddings.shape[0]
    groups, planes = lax.axis_size("label"), lax.axis_size("dp")
    shape = jax.ShapeDtypeStruct
    positive = positive.reshape(1, rows)
    madds = rows * labels * width
    chunk = labels // planes

    given = (shortlist, positive, queries, embeddings)
    (stats,) = call(
        stats_kernel,
        (shape((groups, 2, rows), F32),),
        given,
        flops=2 * madds,
        scratch=[pltpu.VMEM(x.shape, x.dtype) for x in given] + [pltpu.SemaphoreType.DMA((4,))],
        any_inputs=4,
        vmem=VMEM_MOST,
    )
    stats = lax.all_to_all(stats, "label", 0, 0)
    losses, query_part, keep, right, left, far = call(
        gradient_kernel,
        (
            shape((1, rows), F32),
            shape((rows, width), BF16),
            shape((planes // 4, chunk, width), F32),
        )
        + (shape((planes // 4, chunk, width), BF16),) * 3,
        (shortlist, positive, stats, queries, embeddings),
        flops=6 * madds,
        scratch=[pltpu.VMEM((labels, width), F32)],
    )
    far, right, left = moved_by_two(far), moved_by(right, 1), moved_by(left, -1)
    query_parts = lax.all_to_all(
        query_part.reshape(groups, rows // groups, width), "label", 0, 0
    )
    spread, keep, right, left, far = call(
        middle_kernel,
        (shape(query_parts.shape, BF16), shape((chunk, width), F32))
        + (shape((chunk, width), BF16),) * 3,
        (query_parts, keep, right, left, far),
    )
    far, right, left = moved_by(far, 8), moved_by(right, 4), moved_by(left, -4)
    query_grad = lax.all_to_all(spread, "label", 0, 0).reshape(rows, width)
    label_grad, query_grad = call(
        last_kernel,
        (
            shape((BLOCK // planes, labels // BLOCK, width), F32),
            shape((rows, width), BF16),
        ),
        (keep, right, left, far, query_grad),
        scratch=[pltpu.SemaphoreType.DMA],
        any_outputs=1,
    )
    return losses.reshape(rows), query_grad, label_grad


def solution(mesh):
    in_specs = (P("dp", None), P("label", None), P("dp", None), P("dp"))
    out_specs = (P("dp"), P("dp", None), P("dp", "label", None))
    return jax.shard_map(body, mesh=mesh, in_specs=in_specs, out_specs=out_specs, check_vma=False)
```

```python
import jax
import jax.numpy as jnp
from jax import lax
from jax.experimental import pallas as pl
from jax.experimental.pallas import tpu as pltpu
from jax.sharding import PartitionSpec as P

BLOCK = 128
LOWEST = -3.4028234e38
VMEM_LIMIT = 24 * 1024 * 1024
VMEM_MOST = 62_000_000
LONG = 60_000_000_000
F32 = jnp.float32
BF16 = jnp.bfloat16


def call(kernel, out_shape, args, flops=0, scratch=(), any_inputs=0, any_outputs=0, vmem=VMEM_LIMIT):
    specs = [pl.BlockSpec(memory_space=pltpu.HBM)] * any_inputs
    specs += [pl.BlockSpec(memory_space=pltpu.VMEM)] * (len(args) - any_inputs)
    results = [pl.BlockSpec(memory_space=pltpu.VMEM)] * (len(out_shape) - any_outputs)
    results += [pl.BlockSpec(memory_space=pltpu.HBM)] * any_outputs
    return pl.pallas_call(
        kernel,
        out_shape=out_shape,
        in_specs=specs,
        out_specs=tuple(results),
        scratch_shapes=list(scratch),
        compiler_params=pltpu.CompilerParams(vmem_limit_bytes=vmem),
        cost_estimate=pl.CostEstimate(flops=flops, bytes_accessed=2_000_000, transcendentals=0),
    )(*args)


def local_scores(me, short_ref, positive_ref, queries_ref, embeddings_ref):
    labels, rows = embeddings_ref.shape[0], queries_ref.shape[0]
    label_blocks, query_blocks = labels // BLOCK, rows // BLOCK
    scores = lax.dot_general(
        embeddings_ref[...], queries_ref[...], (((1,), (1,)), ((), ())), preferred_element_type=F32
    )
    listed = short_ref[...]
    masked = []
    for b in range(label_blocks):
        hit = jnp.max(
            jnp.where(listed == me * label_blocks + b, 1.0, 0.0).astype(F32), axis=1, keepdims=True
        )
        row = jnp.concatenate(
            [jnp.broadcast_to(hit[q : q + 1], (1, BLOCK)) for q in range(query_blocks)], axis=1
        )
        masked.append(jnp.where(row > 0.5, scores[b * BLOCK : (b + 1) * BLOCK], -jnp.inf))
    masked = jnp.concatenate(masked, axis=0)
    place = positive_ref[...] - me * labels
    is_positive = lax.broadcasted_iota(jnp.int32, (labels, rows), 0) == place
    return scores, masked, is_positive


def stats_kernel(
    short_hbm, positive_hbm, queries_hbm, embeddings_hbm, out_ref,
    short_ref, positive_ref, queries_ref, embeddings_ref, sems,
):
    copies = [
        pltpu.make_async_copy(source, target, sems.at[i])
        for i, (source, target) in enumerate(
            [
                (queries_hbm, queries_ref),
                (embeddings_hbm, embeddings_ref),
                (short_hbm, short_ref),
                (positive_hbm, positive_ref),
            ]
        )
    ]
    for copy in copies:
        copy.start()
    for copy in copies:
        copy.wait()
    me = lax.axis_index("label")
    scores, masked, is_positive = local_scores(
        me, short_ref, positive_ref, queries_ref, embeddings_ref
    )
    top = jnp.maximum(jnp.max(masked, axis=0, keepdims=True), LOWEST)
    total = jnp.sum(jnp.exp(masked - top), axis=0, keepdims=True)
    positive = jnp.sum(jnp.where(is_positive, scores, 0.0), axis=0, keepdims=True)
    rows = jnp.concatenate([top + jnp.log(total), positive], axis=0)
    out_ref[...] = jnp.broadcast_to(rows[None], out_ref.shape)


def gradient_kernel(
    short_ref, positive_ref, stats_ref, queries_ref, embeddings_ref,
    loss_ref, query_ref, keep_ref, right_ref, left_ref, far_ref, part_ref,
):
    me = lax.axis_index("label")
    logs = stats_ref[:, 0, :]
    top = jnp.max(logs, axis=0, keepdims=True)
    log_total = top + jnp.log(jnp.sum(jnp.exp(logs - top), axis=0, keepdims=True))
    positive = jnp.sum(stats_ref[:, 1, :], axis=0, keepdims=True)
    loss_ref[...] = log_total - positive
    _, masked, is_positive = local_scores(me, short_ref, positive_ref, queries_ref, embeddings_ref)
    weights = jnp.exp(masked - log_total)
    gradient = jnp.where(is_positive, weights - 1.0, weights).astype(BF16)
    part_ref[...] = jnp.dot(gradient, queries_ref[...], preferred_element_type=F32)
    plane = lax.axis_index("dp")
    labels = part_ref.shape[0]
    deep = BLOCK // lax.axis_size("dp")
    blocks = labels // BLOCK
    for ref, shift in ((keep_ref, 0), (right_ref, 1), (left_ref, 3), (far_ref, 2)):
        kind = lax.rem(plane + shift, 4)
        for m in range(ref.shape[0]):
            start = pl.multiple_of((4 * m + kind) * deep, deep)
            rows = [part_ref[pl.ds(b * BLOCK + start, deep), :] for b in range(blocks)]
            ref[m] = jnp.concatenate(rows, axis=0).astype(ref.dtype)
    query_ref[...] = lax.dot_general(
        gradient, embeddings_ref[...], (((0,), (0,)), ((), ())), preferred_element_type=F32
    ).astype(BF16)


def spread_kernel(parts_ref, spread_ref):
    total = parts_ref[0].astype(F32)
    for i in range(1, parts_ref.shape[0]):
        total = total + parts_ref[i].astype(F32)
    spread_ref[...] = jnp.broadcast_to(total.astype(BF16)[None], spread_ref.shape)


def middle_kernel(_, a_ref, b_ref, c_ref, d_ref, keep_ref, right_ref, left_ref, far_ref):
    mine = lax.axis_index("dp") // 4
    for ref, shift in ((far_ref, 2), (keep_ref, 0), (right_ref, 1), (left_ref, 3)):
        m = lax.rem(mine + shift, 4)
        total = a_ref[m].astype(F32) + b_ref[m].astype(F32) + c_ref[m].astype(F32) + d_ref[m].astype(F32)
        ref[...] = total.astype(ref.dtype)


def last_kernel(a_ref, b_ref, c_ref, d_ref, query_ref, label_ref, query_hbm, sem):
    copy = pltpu.make_async_copy(query_ref, query_hbm, sem)
    copy.start()
    total = a_ref[...].astype(F32) + b_ref[...].astype(F32) + c_ref[...].astype(F32) + d_ref[...]
    deep, blocks = label_ref.shape[:2]
    for b in range(blocks):
        label_ref[:, b, :] = total[b * deep : (b + 1) * deep]
    copy.wait()


def moved_by(x, shift):
    planes = lax.axis_size("dp")
    return lax.ppermute(x, "dp", [(i, (i + shift) % planes) for i in range(planes)])


def moved_by_two(x):
    planes = lax.axis_size("dp")
    return lax.ppermute(x, "dp", [(i, (i + 2 - i % 2 * 4) % planes) for i in range(planes)])


def body(queries, embeddings, shortlist, positive):
    rows, width = queries.shape
    labels = embeddings.shape[0]
    groups, planes = lax.axis_size("label"), lax.axis_size("dp")
    shape = jax.ShapeDtypeStruct
    positive = positive.reshape(1, rows)
    madds = rows * labels * width
    chunk = labels // planes

    given = (shortlist, positive, queries, embeddings)
    (stats,) = call(
        stats_kernel,
        (shape((groups, 2, rows), F32),),
        given,
        flops=2 * madds,
        scratch=[pltpu.VMEM(x.shape, x.dtype) for x in given] + [pltpu.SemaphoreType.DMA((4,))],
        any_inputs=4,
        vmem=VMEM_MOST,
    )
    stats = lax.all_to_all(stats, "label", 0, 0)
    losses, query_part, keep, right, left, far = call(
        gradient_kernel,
        (
            shape((1, rows), F32),
            shape((rows, width), BF16),
            shape((planes // 4, chunk, width), F32),
        )
        + (shape((planes // 4, chunk, width), BF16),) * 3,
        (shortlist, positive, stats, queries, embeddings),
        flops=6 * madds,
        scratch=[pltpu.VMEM((labels, width), F32)],
    )
    far, right, left = moved_by_two(far), moved_by(right, 1), moved_by(left, -1)
    query_parts = lax.all_to_all(
        query_part.reshape(groups, rows // groups, width), "label", 0, 0
    )
    (spread,) = call(
        spread_kernel, (shape(query_parts.shape, BF16),), (query_parts,), flops=LONG
    )
    query_grad = lax.all_to_all(spread, "label", 0, 0).reshape(rows, width)
    keep, right, left, far = call(
        middle_kernel,
        (shape((chunk, width), F32),) + (shape((chunk, width), BF16),) * 3,
        (spread, far, right, left, keep),
        any_inputs=1,
        flops=LONG,
    )
    far, right, left = moved_by(far, 8), moved_by(right, 4), moved_by(left, -4)
    label_grad, query_grad = call(
        last_kernel,
        (
            shape((BLOCK // planes, labels // BLOCK, width), F32),
            shape((rows, width), BF16),
        ),
        (far, right, left, keep, query_grad),
        scratch=[pltpu.SemaphoreType.DMA],
        any_outputs=1,
    )
    return losses.reshape(rows), query_grad, label_grad


def solution(mesh):
    in_specs = (P("dp", None), P("label", None), P("dp", None), P("dp"))
    out_specs = (P("dp"), P("dp", None), P("dp", "label", None))
    return jax.shard_map(body, mesh=mesh, in_specs=in_specs, out_specs=out_specs, check_vma=False)
```

```python
import jax
import jax.numpy as jnp
from jax import lax
from jax.experimental import pallas as pl
from jax.experimental.pallas import tpu as pltpu
from jax.sharding import PartitionSpec as P

BLOCK = 128
LOWEST = -3.4028234e38
VMEM_LIMIT = 24 * 1024 * 1024
VMEM_MOST = 62_000_000
LONG = 60_000_000_000
PART = 512
F32 = jnp.float32
BF16 = jnp.bfloat16


def call(kernel, out_shape, args, flops=0, scratch=(), any_inputs=0, any_outputs=0, vmem=VMEM_LIMIT):
    specs = [pl.BlockSpec(memory_space=pltpu.HBM)] * any_inputs
    specs += [pl.BlockSpec(memory_space=pltpu.VMEM)] * (len(args) - any_inputs)
    results = [pl.BlockSpec(memory_space=pltpu.VMEM)] * (len(out_shape) - any_outputs)
    results += [pl.BlockSpec(memory_space=pltpu.HBM)] * any_outputs
    return pl.pallas_call(
        kernel,
        out_shape=out_shape,
        in_specs=specs,
        out_specs=tuple(results),
        scratch_shapes=list(scratch),
        compiler_params=pltpu.CompilerParams(vmem_limit_bytes=vmem),
        cost_estimate=pl.CostEstimate(flops=flops, bytes_accessed=2_000_000, transcendentals=0),
    )(*args)


def part_scores(part, short_ref, positive_ref, queries_ref, embeddings_ref):
    columns = slice(part * PART, (part + 1) * PART)
    scores = lax.dot_general(
        embeddings_ref[...], queries_ref[columns, :], (((1,), (1,)), ((), ())), preferred_element_type=F32
    )
    labels = scores.shape[0]
    label_blocks = labels // BLOCK
    first = lax.axis_index("label") * label_blocks
    listed = short_ref[...]
    masked = []
    for b in range(label_blocks):
        hit = jnp.max(jnp.where(listed == first + b, 1.0, 0.0).astype(F32), axis=1, keepdims=True)
        hit = [
            jnp.broadcast_to(hit[q : q + 1], (1, BLOCK))
            for q in range(columns.start // BLOCK, columns.stop // BLOCK)
        ]
        block = scores[b * BLOCK : (b + 1) * BLOCK]
        masked.append(jnp.where(jnp.concatenate(hit, axis=1) > 0.5, block, -jnp.inf))
    place = positive_ref[:, columns] - first * BLOCK
    is_positive = lax.broadcasted_iota(jnp.int32, scores.shape, 0) == place
    return scores, jnp.concatenate(masked, axis=0), is_positive


def stats_kernel(
    short_hbm, positive_hbm, queries_hbm, embeddings_hbm, out_ref,
    short_ref, positive_ref, queries_ref, embeddings_ref, sems,
):
    parts = [slice(q, q + PART) for q in range(0, queries_ref.shape[0], PART)]
    pairs = [(embeddings_hbm, embeddings_ref), (short_hbm, short_ref), (positive_hbm, positive_ref)]
    pairs += [(queries_hbm.at[rows, :], queries_ref.at[rows, :]) for rows in parts]
    copies = [pltpu.make_async_copy(*pair, sems.at[i]) for i, pair in enumerate(pairs)]
    for copy in copies:
        copy.start()
    for copy in copies[:3]:
        copy.wait()
    for i, columns in enumerate(parts):
        copies[3 + i].wait()
        scores, masked, is_positive = part_scores(
            i, short_ref, positive_ref, queries_ref, embeddings_ref
        )
        top = jnp.maximum(jnp.max(masked, axis=0, keepdims=True), LOWEST)
        total = jnp.sum(jnp.exp(masked - top), axis=0, keepdims=True)
        positive = jnp.sum(jnp.where(is_positive, scores, 0.0), axis=0, keepdims=True)
        rows = jnp.concatenate([top + jnp.log(total), positive], axis=0)
        out_ref[:, :, columns] = jnp.broadcast_to(rows[None], (out_ref.shape[0], 2, PART))


def gradient_kernel(
    short_ref, positive_ref, stats_ref, queries_ref, embeddings_ref,
    loss_ref, keep_ref, right_ref, left_ref, far_ref, query_ref, part_ref,
):
    logs = stats_ref[:, 0, :]
    top = jnp.max(logs, axis=0, keepdims=True)
    log_total = top + jnp.log(jnp.sum(jnp.exp(logs - top), axis=0, keepdims=True))
    positive = jnp.sum(stats_ref[:, 1, :], axis=0, keepdims=True)
    loss_ref[...] = log_total - positive
    _, masked, is_positive = part_scores(0, short_ref, positive_ref, queries_ref, embeddings_ref)
    weights = jnp.exp(masked - log_total)
    gradient = jnp.where(is_positive, weights - 1.0, weights)
    part_ref[...] = gradient
    gradient = gradient.astype(BF16)
    plane = lax.axis_index("dp")
    deep = BLOCK // lax.axis_size("dp")
    blocks = part_ref.shape[0] // BLOCK
    odd = 2 * lax.rem(plane, 2)
    results = ((keep_ref, 0), (right_ref, 1 + odd), (left_ref, 3 - odd), (far_ref, 2))
    pieces = []
    for ref, shift in results:
        kind = lax.rem(plane + shift, 4)
        for m in range(ref.shape[0]):
            start = pl.multiple_of((4 * m + kind) * deep, deep)
            pieces += [part_ref[pl.ds(b * BLOCK + start, deep), :] for b in range(blocks)]
    sorted_rows = jnp.concatenate(pieces, axis=0).astype(BF16)
    terms = jnp.dot(sorted_rows, queries_ref[...], preferred_element_type=F32)
    size = terms.shape[0] // 4
    for i, (ref, _) in enumerate(results):
        ref[...] = terms[i * size : (i + 1) * size].reshape(ref.shape).astype(ref.dtype)
    query_ref[...] = lax.dot_general(
        gradient, embeddings_ref[...], (((0,), (0,)), ((), ())), preferred_element_type=F32
    ).astype(BF16)


def spread_kernel(parts_ref, spread_ref):
    total = parts_ref[0].astype(F32)
    for i in range(1, parts_ref.shape[0]):
        total = total + parts_ref[i].astype(F32)
    spread_ref[...] = jnp.broadcast_to(total.astype(BF16)[None], spread_ref.shape)


def middle_kernel(_, a_ref, b_ref, c_ref, d_ref, keep_ref, right_ref, left_ref, far_ref):
    mine = lax.axis_index("dp") // 4
    for ref, flip in ((far_ref, 2), (keep_ref, 0), (right_ref, 1), (left_ref, 3)):
        m = mine ^ flip
        total = a_ref[m].astype(F32) + b_ref[m].astype(F32) + c_ref[m].astype(F32) + d_ref[m].astype(F32)
        ref[...] = total.astype(ref.dtype)


def copy_kernel(from_ref, token_ref, to_hbm, sem):
    copy = pltpu.make_async_copy(from_ref, to_hbm, sem)
    copy.start()
    token_ref[...] = jnp.zeros_like(token_ref)
    copy.wait()


def last_kernel(_, a_ref, b_ref, c_ref, d_ref, label_ref):
    total = a_ref[...].astype(F32) + b_ref[...].astype(F32) + c_ref[...].astype(F32) + d_ref[...]
    deep, blocks = label_ref.shape[:2]
    for b in range(blocks):
        label_ref[:, b, :] = total[b * deep : (b + 1) * deep]


def moved_by(x, shift):
    planes = lax.axis_size("dp")
    return lax.ppermute(x, "dp", [(i, (i + shift) % planes) for i in range(planes)])


def exchanged(x, flip):
    planes = lax.axis_size("dp")
    return lax.ppermute(x, "dp", [(i, i ^ flip) for i in range(planes)])


def beside(x):
    planes = lax.axis_size("dp")
    return lax.ppermute(x, "dp", [(i, (i - 1 + i % 2 * 2) % planes) for i in range(planes)])


def moved_by_two(x):
    planes = lax.axis_size("dp")
    return lax.ppermute(x, "dp", [(i, (i + 2 - i % 2 * 4) % planes) for i in range(planes)])


def body(queries, embeddings, shortlist, positive):
    rows, width = queries.shape
    labels = embeddings.shape[0]
    groups, planes = lax.axis_size("label"), lax.axis_size("dp")
    shape = jax.ShapeDtypeStruct
    positive = positive.reshape(1, rows)
    madds = rows * labels * width
    chunk = labels // planes

    given = (shortlist, positive, queries, embeddings)
    (stats,) = call(
        stats_kernel,
        (shape((groups, 2, rows), F32),),
        given,
        flops=2 * madds,
        scratch=[pltpu.VMEM(x.shape, x.dtype) for x in given] + [pltpu.SemaphoreType.DMA((3 + rows // PART,))],
        any_inputs=4,
        vmem=VMEM_MOST,
    )
    stats = lax.all_to_all(stats, "label", 0, 0)
    losses, keep, right, left, far, query_part = call(
        gradient_kernel,
        (shape((1, rows), F32), shape((planes // 4, chunk, width), F32))
        + (shape((planes // 4, chunk, width), BF16),) * 3
        + (shape((rows, width), BF16),),
        (shortlist, positive, stats, queries, embeddings),
        flops=6 * madds,
        scratch=[
            pltpu.VMEM((labels, rows), F32),
        ],
    )
    far, right, left = moved_by_two(far), exchanged(right, 1), beside(left)
    query_parts = lax.all_to_all(
        query_part.reshape(groups, rows // groups, width), "label", 0, 0
    )
    (spread,) = call(
        spread_kernel, (shape(query_parts.shape, BF16),), (query_parts,), flops=LONG
    )
    query_grad = lax.all_to_all(spread, "label", 0, 0).reshape(rows, width)
    keep, right, left, far = call(
        middle_kernel,
        (shape((chunk, width), F32),) + (shape((chunk, width), BF16),) * 3,
        (spread, far, right, left, keep),
        any_inputs=1,
        flops=LONG,
    )
    far, right, left = exchanged(far, 8), exchanged(right, 4), exchanged(left, 12)
    token, query_grad = call(
        copy_kernel,
        (shape((8, BLOCK), F32), shape((rows, width), BF16)),
        (query_grad,),
        scratch=[pltpu.SemaphoreType.DMA],
        any_outputs=1,
        flops=LONG,
    )
    (label_grad,) = call(
        last_kernel,
        (shape((BLOCK // planes, labels // BLOCK, width), F32),),
        (token, far, right, left, keep),
    )
    return losses.reshape(rows), query_grad, label_grad


def solution(mesh):
    in_specs = (P("dp", None), P("label", None), P("dp", None), P("dp"))
    out_specs = (P("dp"), P("dp", None), P("dp", "label", None))
    return jax.shard_map(body, mesh=mesh, in_specs=in_specs, out_specs=out_specs, check_vma=False)
```

```python
import jax
import jax.numpy as jnp
from jax import lax
from jax.experimental import pallas as pl
from jax.experimental.pallas import tpu as pltpu
from jax.sharding import PartitionSpec as P

BLOCK = 128
LOWEST = -3.4028234e38
VMEM_LIMIT = 24 * 1024 * 1024
VMEM_MOST = 62_000_000
LONG = 60_000_000_000
PIECE = 512
F32 = jnp.float32
BF16 = jnp.bfloat16


def call(kernel, out_shape, args, flops=0, scratch=(), any_inputs=0, any_outputs=0, vmem=VMEM_LIMIT):
    specs = [pl.BlockSpec(memory_space=pltpu.HBM)] * any_inputs
    specs += [pl.BlockSpec(memory_space=pltpu.VMEM)] * (len(args) - any_inputs)
    results = [pl.BlockSpec(memory_space=pltpu.VMEM)] * (len(out_shape) - any_outputs)
    results += [pl.BlockSpec(memory_space=pltpu.HBM)] * any_outputs
    return pl.pallas_call(
        kernel,
        out_shape=out_shape,
        in_specs=specs,
        out_specs=tuple(results),
        scratch_shapes=list(scratch),
        compiler_params=pltpu.CompilerParams(vmem_limit_bytes=vmem),
        cost_estimate=pl.CostEstimate(flops=flops, bytes_accessed=2_000_000, transcendentals=0),
    )(*args)


def local_scores(short_ref, positive_ref, queries_ref, embeddings_ref):
    scores = lax.dot_general(
        embeddings_ref[...], queries_ref[...], (((1,), (1,)), ((), ())), preferred_element_type=F32
    )
    labels, rows = scores.shape
    label_blocks = labels // BLOCK
    first = lax.axis_index("label") * label_blocks
    listed = short_ref[...]
    masked = []
    for b in range(label_blocks):
        hit = jnp.max(jnp.where(listed == first + b, 1.0, 0.0).astype(F32), axis=1, keepdims=True)
        hit = [jnp.broadcast_to(hit[q : q + 1], (1, BLOCK)) for q in range(rows // BLOCK)]
        block = scores[b * BLOCK : (b + 1) * BLOCK]
        masked.append(jnp.where(jnp.concatenate(hit, axis=1) > 0.5, block, -jnp.inf))
    place = positive_ref[...] - first * BLOCK
    is_positive = lax.broadcasted_iota(jnp.int32, scores.shape, 0) == place
    return scores, jnp.concatenate(masked, axis=0), is_positive


def copies_of(pairs, sems):
    cut = []
    for source, target in pairs:
        rows = source.shape[0]
        if rows <= PIECE:
            cut.append((source, target))
        else:
            at = [pl.ds(r, PIECE) for r in range(0, rows, PIECE)]
            cut += [(source.at[rows, :], target.at[rows, :]) for rows in at]
    return [pltpu.make_async_copy(*pair, sems.at[i]) for i, pair in enumerate(cut)]


def stats_kernel(
    short_hbm, positive_hbm, queries_hbm, embeddings_hbm, out_ref,
    short_ref, positive_ref, queries_ref, embeddings_ref, sems,
):
    copies = copies_of(
        [
            (queries_hbm, queries_ref),
            (embeddings_hbm, embeddings_ref),
            (short_hbm, short_ref),
            (positive_hbm, positive_ref),
        ],
        sems,
    )
    for copy in copies:
        copy.start()
    for copy in copies:
        copy.wait()
    scores, masked, is_positive = local_scores(short_ref, positive_ref, queries_ref, embeddings_ref)
    top = jnp.maximum(jnp.max(masked, axis=0, keepdims=True), LOWEST)
    total = jnp.sum(jnp.exp(masked - top), axis=0, keepdims=True)
    positive = jnp.sum(jnp.where(is_positive, scores, 0.0), axis=0, keepdims=True)
    rows = jnp.concatenate([top + jnp.log(total), positive], axis=0)
    out_ref[...] = jnp.broadcast_to(rows[None], out_ref.shape)


def gradient_kernel(
    short_ref, positive_ref, stats_ref, queries_ref, embeddings_ref,
    loss_ref, keep_ref, right_ref, left_ref, far_ref, query_ref, part_ref,
):
    logs = stats_ref[:, 0, :]
    top = jnp.max(logs, axis=0, keepdims=True)
    log_total = top + jnp.log(jnp.sum(jnp.exp(logs - top), axis=0, keepdims=True))
    positive = jnp.sum(stats_ref[:, 1, :], axis=0, keepdims=True)
    loss_ref[...] = log_total - positive
    _, masked, is_positive = local_scores(short_ref, positive_ref, queries_ref, embeddings_ref)
    weights = jnp.exp(masked - log_total)
    gradient = jnp.where(is_positive, weights - 1.0, weights)
    part_ref[...] = gradient
    gradient = gradient.astype(BF16)
    plane = lax.axis_index("dp")
    deep = BLOCK // lax.axis_size("dp")
    blocks = part_ref.shape[0] // BLOCK
    odd = 2 * lax.rem(plane, 2)
    results = ((keep_ref, 0), (right_ref, 1 + odd), (left_ref, 3 - odd), (far_ref, 2))
    pieces = []
    for ref, shift in results:
        kind = lax.rem(plane + shift, 4)
        for m in range(ref.shape[0]):
            start = pl.multiple_of((4 * m + kind) * deep, deep)
            pieces += [part_ref[pl.ds(b * BLOCK + start, deep), :] for b in range(blocks)]
    sorted_rows = jnp.concatenate(pieces, axis=0).astype(BF16)
    terms = jnp.dot(sorted_rows, queries_ref[...], preferred_element_type=F32)
    size = terms.shape[0] // 4
    for i, (ref, _) in enumerate(results):
        ref[...] = terms[i * size : (i + 1) * size].reshape(ref.shape).astype(ref.dtype)
    query_ref[...] = lax.dot_general(
        gradient, embeddings_ref[...], (((0,), (0,)), ((), ())), preferred_element_type=F32
    ).astype(BF16)


def spread_kernel(parts_ref, spread_ref):
    total = parts_ref[0].astype(F32)
    for i in range(1, parts_ref.shape[0]):
        total = total + parts_ref[i].astype(F32)
    spread_ref[...] = jnp.broadcast_to(total.astype(BF16)[None], spread_ref.shape)


def middle_kernel(_, a_ref, b_ref, c_ref, d_ref, send_ref, keep_ref):
    plane = lax.axis_index("dp")
    mine, first = plane // 4, 1 + 2 * lax.rem(plane, 2)
    for ref, masks in ((send_ref, (first, 2)), (keep_ref, (0, 4 - first))):
        for i, mask in enumerate(masks):
            m = mine ^ mask
            total = a_ref[m].astype(F32) + b_ref[m].astype(F32) + c_ref[m].astype(F32) + d_ref[m].astype(F32)
            ref[i] = total.astype(ref.dtype)


def join_kernel(received_ref, keep_ref, send_ref, own_ref):
    own_ref[...] = received_ref[0].astype(F32) + keep_ref[0]
    send_ref[...] = (received_ref[1].astype(F32) + keep_ref[1]).astype(BF16)


def copy_kernel(from_ref, token_ref, to_hbm, sem):
    copy = pltpu.make_async_copy(from_ref, to_hbm, sem)
    copy.start()
    token_ref[...] = jnp.zeros_like(token_ref)
    copy.wait()


def last_kernel(_, received_ref, own_ref, label_ref):
    total = received_ref[...].astype(F32) + own_ref[...]
    deep, blocks = label_ref.shape[:2]
    for b in range(blocks):
        label_ref[:, b, :] = total[b * deep : (b + 1) * deep]


def exchanged(x, even, odd):
    planes = lax.axis_size("dp")
    return lax.ppermute(x, "dp", [(i, i ^ (odd if i % 2 else even)) for i in range(planes)])


def beside(x):
    planes = lax.axis_size("dp")
    return lax.ppermute(x, "dp", [(i, (i - 1 + i % 2 * 2) % planes) for i in range(planes)])


def moved_by_two(x):
    planes = lax.axis_size("dp")
    return lax.ppermute(x, "dp", [(i, (i + 2 - i % 2 * 4) % planes) for i in range(planes)])


def body(queries, embeddings, shortlist, positive):
    rows, width = queries.shape
    labels = embeddings.shape[0]
    groups, planes = lax.axis_size("label"), lax.axis_size("dp")
    shape = jax.ShapeDtypeStruct
    positive = positive.reshape(1, rows)
    madds = rows * labels * width
    chunk = labels // planes

    given = (shortlist, positive, queries, embeddings)
    (stats,) = call(
        stats_kernel,
        (shape((groups, 2, rows), F32),),
        given,
        flops=2 * madds,
        scratch=[pltpu.VMEM(x.shape, x.dtype) for x in given] + [pltpu.SemaphoreType.DMA((2 + (rows + labels) // PIECE,))],
        any_inputs=4,
        vmem=VMEM_MOST,
    )
    stats = lax.all_to_all(stats, "label", 0, 0)
    losses, keep, right, left, far, query_part = call(
        gradient_kernel,
        (shape((1, rows), F32), shape((planes // 4, chunk, width), F32))
        + (shape((planes // 4, chunk, width), BF16),) * 3
        + (shape((rows, width), BF16),),
        (shortlist, positive, stats, queries, embeddings),
        flops=6 * madds,
        scratch=[
            pltpu.VMEM((labels, rows), F32),
        ],
    )
    far, right, left = moved_by_two(far), exchanged(right, 1, 1), beside(left)
    query_parts = lax.all_to_all(
        query_part.reshape(groups, rows // groups, width), "label", 0, 0
    )
    (spread,) = call(
        spread_kernel, (shape(query_parts.shape, BF16),), (query_parts,), flops=LONG
    )
    query_grad = lax.all_to_all(spread, "label", 0, 0).reshape(rows, width)
    send, keep = call(
        middle_kernel,
        (shape((2, chunk, width), BF16), shape((2, chunk, width), F32)),
        (spread, far, right, left, keep),
        any_inputs=1,
        flops=LONG,
    )
    send, own = call(
        join_kernel,
        (shape((chunk, width), BF16), shape((chunk, width), F32)),
        (exchanged(send, 4, 12), keep),
    )
    received = exchanged(send, 12, 4)
    token, query_grad = call(
        copy_kernel,
        (shape((8, BLOCK), F32), shape((rows, width), BF16)),
        (query_grad,),
        scratch=[pltpu.SemaphoreType.DMA],
        any_outputs=1,
        flops=LONG,
    )
    (label_grad,) = call(
        last_kernel,
        (shape((BLOCK // planes, labels // BLOCK, width), F32),),
        (token, received, own),
    )
    return losses.reshape(rows), query_grad, label_grad


def solution(mesh):
    in_specs = (P("dp", None), P("label", None), P("dp", None), P("dp"))
    out_specs = (P("dp"), P("dp", None), P("dp", "label", None))
    return jax.shard_map(body, mesh=mesh, in_specs=in_specs, out_specs=out_specs, check_vma=False)
```

```python
import jax
import jax.numpy as jnp
from jax import lax
from jax.experimental import pallas as pl
from jax.experimental.pallas import tpu as pltpu
from jax.sharding import PartitionSpec as P

BLOCK = 128
LOWEST = -3.4028234e38
VMEM_LIMIT = 24 * 1024 * 1024
VMEM_MOST = 62_000_000
LONG = 60_000_000_000
PIECE = 512
F32 = jnp.float32
BF16 = jnp.bfloat16


def call(kernel, out_shape, args, flops=0, scratch=(), any_inputs=0, any_outputs=0, vmem=VMEM_LIMIT):
    specs = [pl.BlockSpec(memory_space=pltpu.HBM)] * any_inputs
    specs += [pl.BlockSpec(memory_space=pltpu.VMEM)] * (len(args) - any_inputs)
    results = [pl.BlockSpec(memory_space=pltpu.VMEM)] * (len(out_shape) - any_outputs)
    results += [pl.BlockSpec(memory_space=pltpu.HBM)] * any_outputs
    return pl.pallas_call(
        kernel,
        out_shape=out_shape,
        in_specs=specs,
        out_specs=tuple(results),
        scratch_shapes=list(scratch),
        compiler_params=pltpu.CompilerParams(vmem_limit_bytes=vmem),
        cost_estimate=pl.CostEstimate(flops=flops, bytes_accessed=2_000_000, transcendentals=0),
    )(*args)


def local_scores(short_ref, positive_ref, queries_ref, embeddings_ref):
    scores = lax.dot_general(
        embeddings_ref[...], queries_ref[...], (((1,), (1,)), ((), ())), preferred_element_type=F32
    )
    labels, rows = scores.shape
    label_blocks = labels // BLOCK
    first = lax.axis_index("label") * label_blocks
    listed = short_ref[...]
    masked = []
    for b in range(label_blocks):
        hit = jnp.max(jnp.where(listed == first + b, 1.0, 0.0).astype(F32), axis=1, keepdims=True)
        hit = [jnp.broadcast_to(hit[q : q + 1], (1, BLOCK)) for q in range(rows // BLOCK)]
        block = scores[b * BLOCK : (b + 1) * BLOCK]
        masked.append(jnp.where(jnp.concatenate(hit, axis=1) > 0.5, block, -jnp.inf))
    place = positive_ref[...] - first * BLOCK
    is_positive = lax.broadcasted_iota(jnp.int32, scores.shape, 0) == place
    return scores, jnp.concatenate(masked, axis=0), is_positive


def copies_of(pairs, sems):
    cut = []
    for source, target in pairs:
        rows = source.shape[0]
        if rows <= PIECE:
            cut.append((source, target))
        else:
            at = [pl.ds(r, PIECE) for r in range(0, rows, PIECE)]
            cut += [(source.at[rows, :], target.at[rows, :]) for rows in at]
    return [pltpu.make_async_copy(*pair, sems.at[i]) for i, pair in enumerate(cut)]


def stats_kernel(
    short_hbm, positive_hbm, queries_hbm, embeddings_hbm, out_ref,
    short_ref, positive_ref, queries_ref, embeddings_ref, sems,
):
    copies = copies_of(
        [
            (queries_hbm, queries_ref),
            (embeddings_hbm, embeddings_ref),
            (short_hbm, short_ref),
            (positive_hbm, positive_ref),
        ],
        sems,
    )
    for copy in copies:
        copy.start()
    for copy in copies:
        copy.wait()
    scores, masked, is_positive = local_scores(short_ref, positive_ref, queries_ref, embeddings_ref)
    top = jnp.maximum(jnp.max(masked, axis=0, keepdims=True), LOWEST)
    total = jnp.sum(jnp.exp(masked - top), axis=0, keepdims=True)
    positive = jnp.sum(jnp.where(is_positive, scores, 0.0), axis=0, keepdims=True)
    rows = jnp.concatenate([top + jnp.log(total), positive], axis=0)
    out_ref[...] = jnp.broadcast_to(rows[None], out_ref.shape)


def gradient_kernel(
    short_ref, positive_ref, stats_ref, queries_ref, embeddings_ref,
    loss_ref, grad_ref, keep_ref, right_ref, left_ref, far_ref, part_ref,
):
    logs = stats_ref[:, 0, :]
    top = jnp.max(logs, axis=0, keepdims=True)
    log_total = top + jnp.log(jnp.sum(jnp.exp(logs - top), axis=0, keepdims=True))
    positive = jnp.sum(stats_ref[:, 1, :], axis=0, keepdims=True)
    loss_ref[...] = log_total - positive
    _, masked, is_positive = local_scores(short_ref, positive_ref, queries_ref, embeddings_ref)
    weights = jnp.exp(masked - log_total)
    gradient = jnp.where(is_positive, weights - 1.0, weights)
    part_ref[...] = gradient
    grad_ref[...] = gradient.astype(BF16)
    plane = lax.axis_index("dp")
    deep = BLOCK // lax.axis_size("dp")
    blocks = part_ref.shape[0] // BLOCK
    results = ((keep_ref, 0), (right_ref, 1), (left_ref, 3), (far_ref, 2))
    pieces = []
    for ref, shift in results:
        kind = lax.rem(plane, 4) ^ shift
        for m in range(ref.shape[0]):
            start = pl.multiple_of((4 * m + kind) * deep, deep)
            pieces += [part_ref[pl.ds(b * BLOCK + start, deep), :] for b in range(blocks)]
    sorted_rows = jnp.concatenate(pieces, axis=0).astype(BF16)
    terms = jnp.dot(sorted_rows, queries_ref[...], preferred_element_type=F32)
    size = terms.shape[0] // 4
    for i, (ref, _) in enumerate(results):
        ref[...] = terms[i * size : (i + 1) * size].reshape(ref.shape).astype(ref.dtype)


def query_kernel(grad_ref, embeddings_ref, query_ref):
    query_ref[...] = lax.dot_general(
        grad_ref[...], embeddings_ref[...], (((0,), (0,)), ((), ())), preferred_element_type=F32
    ).astype(BF16)


def spread_kernel(_, parts_ref, spread_ref):
    total = parts_ref[0].astype(F32)
    for i in range(1, parts_ref.shape[0]):
        total = total + parts_ref[i].astype(F32)
    spread_ref[...] = jnp.broadcast_to(total.astype(BF16)[None], spread_ref.shape)


def middle_kernel(a_ref, b_ref, c_ref, d_ref, send_ref, keep_ref):
    mine = lax.axis_index("dp") // 4
    for ref, masks in ((send_ref, (1, 2)), (keep_ref, (0, 3))):
        for i, mask in enumerate(masks):
            m = mine ^ mask
            total = a_ref[m].astype(F32) + b_ref[m].astype(F32) + c_ref[m].astype(F32) + d_ref[m].astype(F32)
            ref[i] = total.astype(ref.dtype)


def join_kernel(_, received_ref, keep_ref, send_ref, own_ref):
    own_ref[...] = received_ref[0].astype(F32) + keep_ref[0]
    send_ref[...] = (received_ref[1].astype(F32) + keep_ref[1]).astype(BF16)


def copy_kernel(from_ref, token_ref, to_hbm, sem):
    copy = pltpu.make_async_copy(from_ref, to_hbm, sem)
    copy.start()
    token_ref[...] = jnp.zeros_like(token_ref)
    copy.wait()


def last_kernel(_, received_ref, own_ref, label_ref):
    total = received_ref[...].astype(F32) + own_ref[...]
    deep, blocks = label_ref.shape[:2]
    for b in range(blocks):
        label_ref[:, b, :] = total[b * deep : (b + 1) * deep]


def exchanged(x, flip):
    return lax.ppermute(x, "dp", [(i, i ^ flip) for i in range(lax.axis_size("dp"))])


def body(queries, embeddings, shortlist, positive):
    rows, width = queries.shape
    labels = embeddings.shape[0]
    groups, planes = lax.axis_size("label"), lax.axis_size("dp")
    shape = jax.ShapeDtypeStruct
    positive = positive.reshape(1, rows)
    madds = rows * labels * width
    chunk = labels // planes

    given = (shortlist, positive, queries, embeddings)
    (stats,) = call(
        stats_kernel,
        (shape((groups, 2, rows), F32),),
        given,
        flops=2 * madds,
        scratch=[pltpu.VMEM(x.shape, x.dtype) for x in given] + [pltpu.SemaphoreType.DMA((2 + (rows + labels) // PIECE,))],
        any_inputs=4,
        vmem=VMEM_MOST,
    )
    stats = lax.all_to_all(stats, "label", 0, 0)
    losses, gradient, keep, right, left, far = call(
        gradient_kernel,
        (
            shape((1, rows), F32),
            shape((labels, rows), BF16),
            shape((planes // 4, chunk, width), F32),
        )
        + (shape((planes // 4, chunk, width), BF16),) * 3,
        (shortlist, positive, stats, queries, embeddings),
        flops=4 * madds,
        scratch=[pltpu.VMEM((labels, rows), F32)],
    )
    (query_part,) = call(
        query_kernel, (shape((rows, width), BF16),), (gradient, embeddings), flops=LONG
    )
    far, right, left = exchanged(far, 2), exchanged(right, 1), exchanged(left, 3)
    query_parts = lax.all_to_all(
        query_part.reshape(groups, rows // groups, width), "label", 0, 0
    )
    send, keep = call(
        middle_kernel,
        (shape((2, chunk, width), BF16), shape((2, chunk, width), F32)),
        (far, right, left, keep),
        flops=LONG,
    )
    (spread,) = call(
        spread_kernel, (shape(query_parts.shape, BF16),), (send, query_parts), any_inputs=1, flops=LONG
    )
    query_grad = lax.all_to_all(spread, "label", 0, 0).reshape(rows, width)
    send, own = call(
        join_kernel,
        (shape((chunk, width), BF16), shape((chunk, width), F32)),
        (spread, exchanged(send, 4), keep),
        any_inputs=1,
        flops=LONG,
    )
    received = exchanged(send, 12)
    token, query_grad = call(
        copy_kernel,
        (shape((8, BLOCK), F32), shape((rows, width), BF16)),
        (query_grad,),
        scratch=[pltpu.SemaphoreType.DMA],
        any_outputs=1,
        flops=LONG,
    )
    (label_grad,) = call(
        last_kernel,
        (shape((BLOCK // planes, labels // BLOCK, width), F32),),
        (token, received, own),
    )
    return losses.reshape(rows), query_grad, label_grad


def solution(mesh):
    in_specs = (P("dp", None), P("label", None), P("dp", None), P("dp"))
    out_specs = (P("dp"), P("dp", None), P("dp", "label", None))
    return jax.shard_map(body, mesh=mesh, in_specs=in_specs, out_specs=out_specs, check_vma=False)
```

```python
import jax
import jax.numpy as jnp
from jax import lax
from jax.experimental import pallas as pl
from jax.experimental.pallas import tpu as pltpu
from jax.sharding import PartitionSpec as P

BLOCK = 128
LOWEST = -3.4028234e38
VMEM_LIMIT = 24 * 1024 * 1024
VMEM_MOST = 62_000_000
LONG = 60_000_000_000
PIECE = 512
F32 = jnp.float32
BF16 = jnp.bfloat16


def call(kernel, out_shape, args, flops=0, scratch=(), any_inputs=0, any_outputs=0, vmem=VMEM_LIMIT):
    specs = [pl.BlockSpec(memory_space=pltpu.HBM)] * any_inputs
    specs += [pl.BlockSpec(memory_space=pltpu.VMEM)] * (len(args) - any_inputs)
    results = [pl.BlockSpec(memory_space=pltpu.VMEM)] * (len(out_shape) - any_outputs)
    results += [pl.BlockSpec(memory_space=pltpu.HBM)] * any_outputs
    return pl.pallas_call(
        kernel,
        out_shape=out_shape,
        in_specs=specs,
        out_specs=tuple(results),
        scratch_shapes=list(scratch),
        compiler_params=pltpu.CompilerParams(vmem_limit_bytes=vmem),
        cost_estimate=pl.CostEstimate(flops=flops, bytes_accessed=2_000_000, transcendentals=0),
    )(*args)


def local_scores(short_ref, positive_ref, queries_ref, embeddings_ref):
    scores = lax.dot_general(
        embeddings_ref[...], queries_ref[...], (((1,), (1,)), ((), ())), preferred_element_type=F32
    )
    labels, rows = scores.shape
    label_blocks = labels // BLOCK
    first = lax.axis_index("label") * label_blocks
    listed = short_ref[...]
    masked = []
    for b in range(label_blocks):
        hit = jnp.max(jnp.where(listed == first + b, 1.0, 0.0).astype(F32), axis=1, keepdims=True)
        hit = [jnp.broadcast_to(hit[q : q + 1], (1, BLOCK)) for q in range(rows // BLOCK)]
        block = scores[b * BLOCK : (b + 1) * BLOCK]
        masked.append(jnp.where(jnp.concatenate(hit, axis=1) > 0.5, block, -jnp.inf))
    place = positive_ref[...] - first * BLOCK
    is_positive = lax.broadcasted_iota(jnp.int32, scores.shape, 0) == place
    return scores, jnp.concatenate(masked, axis=0), is_positive


def copies_of(pairs, sems):
    cut = []
    for source, target in pairs:
        rows = source.shape[0]
        if rows <= PIECE:
            cut.append((source, target))
        else:
            at = [pl.ds(r, PIECE) for r in range(0, rows, PIECE)]
            cut += [(source.at[rows, :], target.at[rows, :]) for rows in at]
    return [pltpu.make_async_copy(*pair, sems.at[i]) for i, pair in enumerate(cut)]


def stats_kernel(
    short_hbm, positive_hbm, queries_hbm, embeddings_hbm, out_ref,
    short_ref, positive_ref, queries_ref, embeddings_ref, sems,
):
    copies = copies_of(
        [
            (queries_hbm, queries_ref),
            (embeddings_hbm, embeddings_ref),
            (short_hbm, short_ref),
            (positive_hbm, positive_ref),
        ],
        sems,
    )
    for copy in copies:
        copy.start()
    for copy in copies:
        copy.wait()
    scores, masked, is_positive = local_scores(short_ref, positive_ref, queries_ref, embeddings_ref)
    top = jnp.maximum(jnp.max(masked, axis=0, keepdims=True), LOWEST)
    total = jnp.sum(jnp.exp(masked - top), axis=0, keepdims=True)
    positive = jnp.sum(jnp.where(is_positive, scores, 0.0), axis=0, keepdims=True)
    rows = jnp.concatenate([top + jnp.log(total), positive], axis=0)
    out_ref[...] = jnp.broadcast_to(rows[None], out_ref.shape)


def log_total_of(stats_ref):
    logs = stats_ref[:, 0, :]
    top = jnp.max(logs, axis=0, keepdims=True)
    return top + jnp.log(jnp.sum(jnp.exp(logs - top), axis=0, keepdims=True))


def gradient_kernel(
    short_ref, positive_ref, stats_ref, queries_ref, embeddings_ref,
    grad_ref, keep_ref, right_ref, left_ref, far_ref, part_ref,
):
    log_total = log_total_of(stats_ref)
    _, masked, is_positive = local_scores(short_ref, positive_ref, queries_ref, embeddings_ref)
    weights = jnp.exp(masked - log_total)
    gradient = jnp.where(is_positive, weights - 1.0, weights)
    part_ref[...] = gradient
    grad_ref[...] = gradient.astype(BF16)
    plane = lax.axis_index("dp")
    deep = BLOCK // lax.axis_size("dp")
    blocks = part_ref.shape[0] // BLOCK
    results = ((keep_ref, 0), (right_ref, 1), (left_ref, 3), (far_ref, 2))
    pieces = []
    for ref, shift in results:
        kind = lax.rem(plane, 4) ^ shift
        for m in range(ref.shape[0]):
            start = pl.multiple_of((4 * m + kind) * deep, deep)
            pieces += [part_ref[pl.ds(b * BLOCK + start, deep), :] for b in range(blocks)]
    sorted_rows = jnp.concatenate(pieces, axis=0).astype(BF16)
    terms = jnp.dot(sorted_rows, queries_ref[...], preferred_element_type=F32)
    size = terms.shape[0] // 4
    for i, (ref, _) in enumerate(results):
        ref[...] = terms[i * size : (i + 1) * size].reshape(ref.shape).astype(ref.dtype)


def query_kernel(grad_ref, embeddings_ref, stats_ref, query_ref, loss_ref):
    loss_ref[...] = log_total_of(stats_ref) - jnp.sum(stats_ref[:, 1, :], axis=0, keepdims=True)
    query_ref[...] = lax.dot_general(
        grad_ref[...], embeddings_ref[...], (((0,), (0,)), ((), ())), preferred_element_type=F32
    ).astype(BF16)


def spread_kernel(_, parts_ref, spread_ref):
    total = parts_ref[0].astype(F32)
    for i in range(1, parts_ref.shape[0]):
        total = total + parts_ref[i].astype(F32)
    spread_ref[...] = jnp.broadcast_to(total.astype(BF16)[None], spread_ref.shape)


def middle_kernel(a_ref, b_ref, c_ref, d_ref, send_ref, keep_ref):
    mine = lax.axis_index("dp") // 4
    for ref, masks in ((send_ref, (1, 2)), (keep_ref, (0, 3))):
        for i, mask in enumerate(masks):
            m = mine ^ mask
            total = a_ref[m].astype(F32) + b_ref[m].astype(F32) + c_ref[m].astype(F32) + d_ref[m].astype(F32)
            ref[i] = total.astype(ref.dtype)


def join_kernel(_, received_ref, keep_ref, send_ref, own_ref):
    own_ref[...] = received_ref[0].astype(F32) + keep_ref[0]
    send_ref[...] = (received_ref[1].astype(F32) + keep_ref[1]).astype(BF16)


def copy_kernel(from_ref, token_ref, to_hbm, sem):
    copy = pltpu.make_async_copy(from_ref, to_hbm, sem)
    copy.start()
    token_ref[...] = jnp.zeros_like(token_ref)
    copy.wait()


def last_kernel(_, received_ref, own_ref, label_ref):
    total = received_ref[...].astype(F32) + own_ref[...]
    deep, blocks = label_ref.shape[:2]
    for b in range(blocks):
        label_ref[:, b, :] = total[b * deep : (b + 1) * deep]


def exchanged(x, flip):
    return lax.ppermute(x, "dp", [(i, i ^ flip) for i in range(lax.axis_size("dp"))])


def body(queries, embeddings, shortlist, positive):
    rows, width = queries.shape
    labels = embeddings.shape[0]
    groups, planes = lax.axis_size("label"), lax.axis_size("dp")
    shape = jax.ShapeDtypeStruct
    positive = positive.reshape(1, rows)
    madds = rows * labels * width
    chunk = labels // planes

    given = (shortlist, positive, queries, embeddings)
    (stats,) = call(
        stats_kernel,
        (shape((groups, 2, rows), F32),),
        given,
        flops=2 * madds,
        scratch=[pltpu.VMEM(x.shape, x.dtype) for x in given] + [pltpu.SemaphoreType.DMA((2 + (rows + labels) // PIECE,))],
        any_inputs=4,
        vmem=VMEM_MOST,
    )
    stats = lax.all_to_all(stats, "label", 0, 0)
    gradient, keep, right, left, far = call(
        gradient_kernel,
        (
            shape((labels, rows), BF16),
            shape((planes // 4, chunk, width), F32),
        )
        + (shape((planes // 4, chunk, width), BF16),) * 3,
        (shortlist, positive, stats, queries, embeddings),
        flops=4 * madds,
        scratch=[pltpu.VMEM((labels, rows), F32)],
    )
    query_part, losses = call(
        query_kernel,
        (shape((rows, width), BF16), shape((1, rows), F32)),
        (gradient, embeddings, stats),
        flops=LONG,
    )
    far, right, left = exchanged(far, 2), exchanged(right, 1), exchanged(left, 3)
    query_parts = lax.all_to_all(
        query_part.reshape(groups, rows // groups, width), "label", 0, 0
    )
    send, keep = call(
        middle_kernel,
        (shape((2, chunk, width), BF16), shape((2, chunk, width), F32)),
        (far, right, left, keep),
        flops=LONG,
    )
    (spread,) = call(
        spread_kernel, (shape(query_parts.shape, BF16),), (send, query_parts), any_inputs=1, flops=LONG
    )
    query_grad = lax.all_to_all(spread, "label", 0, 0).reshape(rows, width)
    send, own = call(
        join_kernel,
        (shape((chunk, width), BF16), shape((chunk, width), F32)),
        (spread, exchanged(send, 4), keep),
        any_inputs=1,
        flops=LONG,
    )
    received = exchanged(send, 12)
    token, query_grad = call(
        copy_kernel,
        (shape((8, BLOCK), F32), shape((rows, width), BF16)),
        (query_grad,),
        scratch=[pltpu.SemaphoreType.DMA],
        any_outputs=1,
        flops=LONG,
    )
    (label_grad,) = call(
        last_kernel,
        (shape((BLOCK // planes, labels // BLOCK, width), F32),),
        (token, received, own),
    )
    return losses.reshape(rows), query_grad, label_grad


def solution(mesh):
    in_specs = (P("dp", None), P("label", None), P("dp", None), P("dp"))
    out_specs = (P("dp"), P("dp", None), P("dp", "label", None))
    return jax.shard_map(body, mesh=mesh, in_specs=in_specs, out_specs=out_specs, check_vma=False)
```

```python
import jax
import jax.numpy as jnp
from jax import lax
from jax.experimental import pallas as pl
from jax.experimental.pallas import tpu as pltpu
from jax.sharding import PartitionSpec as P

BLOCK = 128
LOWEST = -3.4028234e38
VMEM_LIMIT = 24 * 1024 * 1024
VMEM_MOST = 62_000_000
LONG = 60_000_000_000
PIECE = 512
F32 = jnp.float32
BF16 = jnp.bfloat16


def call(kernel, out_shape, args, flops=0, scratch=(), any_inputs=0, any_outputs=0, vmem=VMEM_LIMIT):
    specs = [pl.BlockSpec(memory_space=pltpu.HBM)] * any_inputs
    specs += [pl.BlockSpec(memory_space=pltpu.VMEM)] * (len(args) - any_inputs)
    results = [pl.BlockSpec(memory_space=pltpu.VMEM)] * (len(out_shape) - any_outputs)
    results += [pl.BlockSpec(memory_space=pltpu.HBM)] * any_outputs
    return pl.pallas_call(
        kernel,
        out_shape=out_shape,
        in_specs=specs,
        out_specs=tuple(results),
        scratch_shapes=list(scratch),
        compiler_params=pltpu.CompilerParams(vmem_limit_bytes=vmem),
        cost_estimate=pl.CostEstimate(flops=flops, bytes_accessed=2_000_000, transcendentals=0),
    )(*args)


def local_scores(short_ref, positive_ref, queries_ref, embeddings_ref):
    scores = lax.dot_general(
        embeddings_ref[...], queries_ref[...], (((1,), (1,)), ((), ())), preferred_element_type=F32
    )
    labels, rows = scores.shape
    label_blocks = labels // BLOCK
    first = lax.axis_index("label") * label_blocks
    listed = short_ref[...]
    masked = []
    for b in range(label_blocks):
        hit = jnp.max(jnp.where(listed == first + b, 1.0, 0.0).astype(F32), axis=1, keepdims=True)
        hit = [jnp.broadcast_to(hit[q : q + 1], (1, BLOCK)) for q in range(rows // BLOCK)]
        block = scores[b * BLOCK : (b + 1) * BLOCK]
        masked.append(jnp.where(jnp.concatenate(hit, axis=1) > 0.5, block, -jnp.inf))
    place = positive_ref[...] - first * BLOCK
    is_positive = lax.broadcasted_iota(jnp.int32, scores.shape, 0) == place
    return scores, jnp.concatenate(masked, axis=0), is_positive


def copies_of(pairs, sems):
    cut = []
    for source, target in pairs:
        rows = source.shape[0]
        if rows <= PIECE:
            cut.append((source, target))
        else:
            at = [pl.ds(r, PIECE) for r in range(0, rows, PIECE)]
            cut += [(source.at[rows, :], target.at[rows, :]) for rows in at]
    return [pltpu.make_async_copy(*pair, sems.at[i]) for i, pair in enumerate(cut)]


def stats_kernel(
    short_hbm, positive_hbm, queries_hbm, embeddings_hbm, out_ref,
    short_ref, positive_ref, queries_ref, embeddings_ref, sems,
):
    copies = copies_of(
        [
            (queries_hbm, queries_ref),
            (embeddings_hbm, embeddings_ref),
            (short_hbm, short_ref),
            (positive_hbm, positive_ref),
        ],
        sems,
    )
    for copy in copies:
        copy.start()
    for copy in copies:
        copy.wait()
    scores, masked, is_positive = local_scores(short_ref, positive_ref, queries_ref, embeddings_ref)
    top = jnp.maximum(jnp.max(masked, axis=0, keepdims=True), LOWEST)
    total = jnp.sum(jnp.exp(masked - top), axis=0, keepdims=True)
    positive = jnp.sum(jnp.where(is_positive, scores, 0.0), axis=0, keepdims=True)
    rows = jnp.concatenate([top + jnp.log(total), positive], axis=0)
    out_ref[...] = jnp.broadcast_to(rows[None], out_ref.shape)


def log_total_of(stats_ref):
    logs = stats_ref[:, 0, :]
    top = jnp.max(logs, axis=0, keepdims=True)
    return top + jnp.log(jnp.sum(jnp.exp(logs - top), axis=0, keepdims=True))


def gradient_kernel(
    short_ref, positive_ref, stats_ref, queries_ref, embeddings_ref,
    grad_ref, keep_ref, right_ref, left_ref, far_ref, part_ref,
):
    log_total = log_total_of(stats_ref)
    _, masked, is_positive = local_scores(short_ref, positive_ref, queries_ref, embeddings_ref)
    weights = jnp.exp(masked - log_total)
    gradient = jnp.where(is_positive, weights - 1.0, weights)
    part_ref[...] = gradient
    grad_ref[...] = gradient.astype(BF16)
    plane = lax.axis_index("dp")
    deep = BLOCK // lax.axis_size("dp")
    blocks = part_ref.shape[0] // BLOCK
    results = ((keep_ref, 0), (right_ref, 1), (left_ref, 3), (far_ref, 2))
    pieces = []
    for ref, shift in results:
        kind = lax.rem(plane, 4) ^ shift
        for m in range(ref.shape[0]):
            start = pl.multiple_of((4 * m + kind) * deep, deep)
            pieces += [part_ref[pl.ds(b * BLOCK + start, deep), :] for b in range(blocks)]
    sorted_rows = jnp.concatenate(pieces, axis=0).astype(BF16)
    terms = jnp.dot(sorted_rows, queries_ref[...], preferred_element_type=F32)
    size = terms.shape[0] // 4
    for i, (ref, _) in enumerate(results):
        ref[...] = terms[i * size : (i + 1) * size].reshape(ref.shape).astype(ref.dtype)


def query_kernel(grad_ref, embeddings_ref, stats_ref, query_ref, loss_ref):
    loss_ref[...] = log_total_of(stats_ref) - jnp.sum(stats_ref[:, 1, :], axis=0, keepdims=True)
    query_ref[...] = lax.dot_general(
        grad_ref[...], embeddings_ref[...], (((0,), (0,)), ((), ())), preferred_element_type=F32
    ).astype(BF16)


def spread_kernel(_, parts_ref, spread_ref):
    total = parts_ref[0].astype(F32)
    for i in range(1, parts_ref.shape[0]):
        total = total + parts_ref[i].astype(F32)
    spread_ref[...] = jnp.broadcast_to(total.astype(BF16)[None], spread_ref.shape)


def middle_kernel(a_ref, b_ref, c_ref, d_ref, send_ref, keep_ref):
    mine = lax.axis_index("dp") // 4
    for ref, masks in ((send_ref, (1, 2)), (keep_ref, (0, 3))):
        for i, mask in enumerate(masks):
            m = mine ^ mask
            total = a_ref[m].astype(F32) + b_ref[m].astype(F32) + c_ref[m].astype(F32) + d_ref[m].astype(F32)
            ref[i] = total.astype(ref.dtype)


def join_kernel(_, received_ref, keep_ref, send_ref, own_ref):
    own_ref[...] = received_ref[0].astype(F32) + keep_ref[0]
    send_ref[...] = (received_ref[1].astype(F32) + keep_ref[1]).astype(BF16)


def last_kernel(query_ref, received_ref, own_ref, query_hbm, label_hbm, label_ref, sems):
    query_copy = pltpu.make_async_copy(query_ref, query_hbm, sems.at[0])
    query_copy.start()
    total = received_ref[...].astype(F32) + own_ref[...]
    deep, blocks = label_ref.shape[:2]
    for b in range(blocks):
        label_ref[:, b, :] = total[b * deep : (b + 1) * deep]
    label_copy = pltpu.make_async_copy(label_ref, label_hbm, sems.at[1])
    label_copy.start()
    label_copy.wait()
    query_copy.wait()


def exchanged(x, flip):
    return lax.ppermute(x, "dp", [(i, i ^ flip) for i in range(lax.axis_size("dp"))])


def body(queries, embeddings, shortlist, positive):
    rows, width = queries.shape
    labels = embeddings.shape[0]
    groups, planes = lax.axis_size("label"), lax.axis_size("dp")
    shape = jax.ShapeDtypeStruct
    positive = positive.reshape(1, rows)
    madds = rows * labels * width
    chunk = labels // planes

    given = (shortlist, positive, queries, embeddings)
    (stats,) = call(
        stats_kernel,
        (shape((groups, 2, rows), F32),),
        given,
        flops=2 * madds,
        scratch=[pltpu.VMEM(x.shape, x.dtype) for x in given] + [pltpu.SemaphoreType.DMA((2 + (rows + labels) // PIECE,))],
        any_inputs=4,
        vmem=VMEM_MOST,
    )
    stats = lax.all_to_all(stats, "label", 0, 0)
    gradient, keep, right, left, far = call(
        gradient_kernel,
        (
            shape((labels, rows), BF16),
            shape((planes // 4, chunk, width), F32),
        )
        + (shape((planes // 4, chunk, width), BF16),) * 3,
        (shortlist, positive, stats, queries, embeddings),
        flops=4 * madds,
        scratch=[pltpu.VMEM((labels, rows), F32)],
    )
    query_part, losses = call(
        query_kernel,
        (shape((rows, width), BF16), shape((1, rows), F32)),
        (gradient, embeddings, stats),
        flops=LONG,
    )
    far, right, left = exchanged(far, 2), exchanged(right, 1), exchanged(left, 3)
    query_parts = lax.all_to_all(
        query_part.reshape(groups, rows // groups, width), "label", 0, 0
    )
    send, keep = call(
        middle_kernel,
        (shape((2, chunk, width), BF16), shape((2, chunk, width), F32)),
        (far, right, left, keep),
        flops=LONG,
    )
    (spread,) = call(
        spread_kernel, (shape(query_parts.shape, BF16),), (send, query_parts), any_inputs=1, flops=LONG
    )
    query_grad = lax.all_to_all(spread, "label", 0, 0).reshape(rows, width)
    send, own = call(
        join_kernel,
        (shape((chunk, width), BF16), shape((chunk, width), F32)),
        (spread, exchanged(send, 4), keep),
        any_inputs=1,
        flops=LONG,
    )
    received = exchanged(send, 12)
    label_shape = (BLOCK // planes, labels // BLOCK, width)
    query_grad, label_grad = call(
        last_kernel,
        (shape((rows, width), BF16), shape(label_shape, F32)),
        (query_grad, received, own),
        scratch=[pltpu.VMEM(label_shape, F32), pltpu.SemaphoreType.DMA((2,))],
        any_outputs=2,
    )
    return losses.reshape(rows), query_grad, label_grad


def solution(mesh):
    in_specs = (P("dp", None), P("label", None), P("dp", None), P("dp"))
    out_specs = (P("dp"), P("dp", None), P("dp", "label", None))
    return jax.shard_map(body, mesh=mesh, in_specs=in_specs, out_specs=out_specs, check_vma=False)
```

```python
import jax
import jax.numpy as jnp
from jax import lax
from jax.experimental import pallas as pl
from jax.experimental.pallas import tpu as pltpu
from jax.sharding import PartitionSpec as P

BLOCK = 128
LOWEST = -3.4028234e38
VMEM_LIMIT = 24 * 1024 * 1024
VMEM_MOST = 62_000_000
LONG = 60_000_000_000
PIECE = 512
F32 = jnp.float32
BF16 = jnp.bfloat16


def call(kernel, out_shape, args, flops=0, scratch=(), any_inputs=0, any_outputs=0, vmem=VMEM_LIMIT):
    specs = [pl.BlockSpec(memory_space=pltpu.HBM)] * any_inputs
    specs += [pl.BlockSpec(memory_space=pltpu.VMEM)] * (len(args) - any_inputs)
    results = [pl.BlockSpec(memory_space=pltpu.VMEM)] * (len(out_shape) - any_outputs)
    results += [pl.BlockSpec(memory_space=pltpu.HBM)] * any_outputs
    return pl.pallas_call(
        kernel,
        out_shape=out_shape,
        in_specs=specs,
        out_specs=tuple(results),
        scratch_shapes=list(scratch),
        compiler_params=pltpu.CompilerParams(vmem_limit_bytes=vmem),
        cost_estimate=pl.CostEstimate(flops=flops, bytes_accessed=2_000_000, transcendentals=0),
    )(*args)


def local_scores(short_ref, positive_ref, queries_ref, embeddings_ref):
    scores = lax.dot_general(
        embeddings_ref[...], queries_ref[...], (((1,), (1,)), ((), ())), preferred_element_type=F32
    )
    labels, rows = scores.shape
    label_blocks = labels // BLOCK
    first = lax.axis_index("label") * label_blocks
    listed = short_ref[...]
    masked = []
    for b in range(label_blocks):
        hit = jnp.max(jnp.where(listed == first + b, 1.0, 0.0).astype(F32), axis=1, keepdims=True)
        hit = [jnp.broadcast_to(hit[q : q + 1], (1, BLOCK)) for q in range(rows // BLOCK)]
        block = scores[b * BLOCK : (b + 1) * BLOCK]
        masked.append(jnp.where(jnp.concatenate(hit, axis=1) > 0.5, block, -jnp.inf))
    place = positive_ref[...] - first * BLOCK
    is_positive = lax.broadcasted_iota(jnp.int32, scores.shape, 0) == place
    return scores, jnp.concatenate(masked, axis=0), is_positive


def copies_of(pairs, sems):
    cut = []
    for source, target in pairs:
        rows = source.shape[0]
        if rows <= PIECE:
            cut.append((source, target))
        else:
            at = [pl.ds(r, PIECE) for r in range(0, rows, PIECE)]
            cut += [(source.at[rows, :], target.at[rows, :]) for rows in at]
    return [pltpu.make_async_copy(*pair, sems.at[i]) for i, pair in enumerate(cut)]


def stats_kernel(
    short_hbm, positive_hbm, queries_hbm, embeddings_hbm, out_ref,
    short_ref, positive_ref, queries_ref, embeddings_ref, sems,
):
    copies = copies_of(
        [
            (queries_hbm, queries_ref),
            (embeddings_hbm, embeddings_ref),
            (short_hbm, short_ref),
            (positive_hbm, positive_ref),
        ],
        sems,
    )
    for copy in copies:
        copy.start()
    for copy in copies:
        copy.wait()
    scores, masked, is_positive = local_scores(short_ref, positive_ref, queries_ref, embeddings_ref)
    top = jnp.maximum(jnp.max(masked, axis=0, keepdims=True), LOWEST)
    total = jnp.sum(jnp.exp(masked - top), axis=0, keepdims=True)
    positive = jnp.sum(jnp.where(is_positive, scores, 0.0), axis=0, keepdims=True)
    rows = jnp.concatenate([top + jnp.log(total), positive], axis=0)
    out_ref[...] = jnp.broadcast_to(rows[None], out_ref.shape)


def log_total_of(stats_ref):
    both = stats_ref[...]
    top = jnp.max(both, axis=0)
    return (top + jnp.log(jnp.sum(jnp.exp(both - top[None]), axis=0)))[0:1]


def gradient_kernel(
    short_ref, positive_ref, stats_ref, queries_ref, embeddings_ref,
    grad_ref, keep_ref, right_ref, left_ref, far_ref, part_ref,
):
    log_total = log_total_of(stats_ref)
    _, masked, is_positive = local_scores(short_ref, positive_ref, queries_ref, embeddings_ref)
    weights = jnp.exp(masked - log_total)
    gradient = jnp.where(is_positive, weights - 1.0, weights)
    part_ref[...] = gradient
    grad_ref[...] = gradient.astype(BF16)
    plane = lax.axis_index("dp")
    deep = BLOCK // lax.axis_size("dp")
    blocks = part_ref.shape[0] // BLOCK
    results = ((keep_ref, 0), (right_ref, 1), (left_ref, 3), (far_ref, 2))
    pieces = []
    for ref, shift in results:
        kind = lax.rem(plane, 4) ^ shift
        for m in range(ref.shape[0]):
            start = pl.multiple_of((4 * m + kind) * deep, deep)
            pieces += [part_ref[pl.ds(b * BLOCK + start, deep), :] for b in range(blocks)]
    sorted_rows = jnp.concatenate(pieces, axis=0).astype(BF16)
    terms = jnp.dot(sorted_rows, queries_ref[...], preferred_element_type=F32)
    size = terms.shape[0] // 4
    for i, (ref, _) in enumerate(results):
        ref[...] = terms[i * size : (i + 1) * size].reshape(ref.shape).astype(ref.dtype)


def query_kernel(grad_ref, embeddings_ref, stats_ref, query_ref, loss_ref):
    loss_ref[...] = log_total_of(stats_ref) - jnp.sum(stats_ref[:, 1, :], axis=0, keepdims=True)
    query_ref[...] = lax.dot_general(
        grad_ref[...], embeddings_ref[...], (((0,), (0,)), ((), ())), preferred_element_type=F32
    ).astype(BF16)


def spread_kernel(_, parts_ref, spread_ref):
    total = parts_ref[0].astype(F32)
    for i in range(1, parts_ref.shape[0]):
        total = total + parts_ref[i].astype(F32)
    spread_ref[...] = jnp.broadcast_to(total.astype(BF16)[None], spread_ref.shape)


def middle_kernel(a_ref, b_ref, c_ref, d_ref, send_ref, keep_ref):
    mine = lax.axis_index("dp") // 4
    for ref, masks in ((send_ref, (1, 2)), (keep_ref, (0, 3))):
        for i, mask in enumerate(masks):
            m = mine ^ mask
            total = a_ref[m].astype(F32) + b_ref[m].astype(F32) + c_ref[m].astype(F32) + d_ref[m].astype(F32)
            ref[i] = total.astype(ref.dtype)


def join_kernel(_, received_ref, keep_ref, send_ref, own_ref):
    own_ref[...] = received_ref[0].astype(F32) + keep_ref[0]
    send_ref[...] = (received_ref[1].astype(F32) + keep_ref[1]).astype(BF16)


def last_kernel(query_ref, received_ref, own_ref, query_hbm, label_hbm, label_ref, sems):
    query_copy = pltpu.make_async_copy(query_ref, query_hbm, sems.at[0])
    query_copy.start()
    total = received_ref[...].astype(F32) + own_ref[...]
    deep, blocks = label_ref.shape[:2]
    for b in range(blocks):
        label_ref[:, b, :] = total[b * deep : (b + 1) * deep]
    label_copy = pltpu.make_async_copy(label_ref, label_hbm, sems.at[1])
    label_copy.start()
    label_copy.wait()
    query_copy.wait()


def exchanged(x, flip):
    return lax.ppermute(x, "dp", [(i, i ^ flip) for i in range(lax.axis_size("dp"))])


def body(queries, embeddings, shortlist, positive):
    rows, width = queries.shape
    labels = embeddings.shape[0]
    groups, planes = lax.axis_size("label"), lax.axis_size("dp")
    shape = jax.ShapeDtypeStruct
    positive = positive.reshape(1, rows)
    madds = rows * labels * width
    chunk = labels // planes

    given = (shortlist, positive, queries, embeddings)
    (stats,) = call(
        stats_kernel,
        (shape((groups, 2, rows), F32),),
        given,
        flops=2 * madds,
        scratch=[pltpu.VMEM(x.shape, x.dtype) for x in given] + [pltpu.SemaphoreType.DMA((2 + (rows + labels) // PIECE,))],
        any_inputs=4,
        vmem=VMEM_MOST,
    )
    stats = lax.all_to_all(stats, "label", 0, 0)
    gradient, keep, right, left, far = call(
        gradient_kernel,
        (
            shape((labels, rows), BF16),
            shape((planes // 4, chunk, width), F32),
        )
        + (shape((planes // 4, chunk, width), BF16),) * 3,
        (shortlist, positive, stats, queries, embeddings),
        flops=4 * madds,
        scratch=[pltpu.VMEM((labels, rows), F32)],
    )
    query_part, losses = call(
        query_kernel,
        (shape((rows, width), BF16), shape((1, rows), F32)),
        (gradient, embeddings, stats),
        flops=LONG,
    )
    far, right, left = exchanged(far, 2), exchanged(right, 1), exchanged(left, 3)
    query_parts = lax.all_to_all(
        query_part.reshape(groups, rows // groups, width), "label", 0, 0
    )
    send, keep = call(
        middle_kernel,
        (shape((2, chunk, width), BF16), shape((2, chunk, width), F32)),
        (far, right, left, keep),
        flops=LONG,
    )
    (spread,) = call(
        spread_kernel, (shape(query_parts.shape, BF16),), (send, query_parts), any_inputs=1, flops=LONG
    )
    query_grad = lax.all_to_all(spread, "label", 0, 0).reshape(rows, width)
    send, own = call(
        join_kernel,
        (shape((chunk, width), BF16), shape((chunk, width), F32)),
        (spread, exchanged(send, 4), keep),
        any_inputs=1,
        flops=LONG,
    )
    received = exchanged(send, 12)
    label_shape = (BLOCK // planes, labels // BLOCK, width)
    query_grad, label_grad = call(
        last_kernel,
        (shape((rows, width), BF16), shape(label_shape, F32)),
        (query_grad, received, own),
        scratch=[pltpu.VMEM(label_shape, F32), pltpu.SemaphoreType.DMA((2,))],
        any_outputs=2,
    )
    return losses.reshape(rows), query_grad, label_grad


def solution(mesh):
    in_specs = (P("dp", None), P("label", None), P("dp", None), P("dp"))
    out_specs = (P("dp"), P("dp", None), P("dp", "label", None))
    return jax.shard_map(body, mesh=mesh, in_specs=in_specs, out_specs=out_specs, check_vma=False)
```
